512 devices in a mesh: grp: 4 (over y), clu: 128 (over x, z, core).
Axes of the slice: x: 4, y: 4, z: 16, core: 2. Of those that a mesh axis runs over, the one named last changes fastest.
Arguments:
- forces: bfloat16 [3, 32768, 512], P(None, 'clu'), may hold values from -6 to 6
- order: int32 [32768], P('clu'), may hold values from 0 to 32767, as said below
- bases: bfloat16 [2, 32, 3, 32768], P(None, None, None, 'clu'), may hold values from -0.21875 to 0.21875
- near_tiles: bfloat16 [128, 8, 768, 768], P('clu', 'grp'), may hold values from -0.078125 to 0.078125
- near_col: int32 [128, 8], P('clu', 'grp'), may hold values from 0 to 127, as said below
- far_basis: bfloat16 [128, 64, 32, 768], P('clu', 'grp'), may hold values from -0.03125 to 0.03125
- far_coupling: bfloat16 [128, 64, 32, 32], P('clu', 'grp'), may hold values from -1 to 1
- far_scale: float32 [128, 64], P('clu', 'grp'), may hold values from 0.5 to 2
- far_rank: int32 [128, 64], P('clu', 'grp'), may hold values from 8 to 32
- far_target: int32 [128, 64], P('clu', 'grp'), may hold values from 0 to 5, as said below
Outputs:
- velocity: float32 [3, 32768, 512], P(None, 'clu', 'grp')
The draws below stay inside these ranges and needn't reach their ends.
Inputs may be any that keep to these rules, and one draw needn't show every extreme that they name: `order`: A permutation of the bead numbers; the 256 positions of row block c hold beads of chain blocks c - 1, c and c + 1 only, counted cyclically, exactly 64 of them from chain block c - 1 and exactly 64 from chain block c + 1. `near_col`: each near tile's column block lies within two blocks of its row block, counted cyclically. `far_target`: level l takes indices 2 ** (l + 1) - 2 to 2 ** (l + 2) - 3; the named cluster never contains the block's own row block.
All inputs are finite; a program needn't handle non-finite values.
Results may differ from the reference program's by a relative error of at most 0.0025.
Values may be sent and summed in bfloat16 or wider, within the bound.
No kernel may reach another device: no remote copies, remote signals or barrier semaphores. Data moves between devices by JAX's collectives and lax.ppermute only.
A program may use at most 64 MiB of HBM per device.

```python
import math
import jax
import jax.numpy as jnp
from jax import lax

TILE = 256
RANK = 32
LEVELS = 2
NRHS = 512
FAR_DEV = 16
N_BEADS = 32768
NEARS = 8
FARS = 64
N_CLU = 128


def draw_order(key, part):
    clusters = N_BEADS // TILE
    quarter = TILE // 4
    first_key, second_key = jax.random.split(jax.random.fold_in(key, 11))
    chain_perm = jax.vmap(lambda k: jax.random.permutation(k, TILE))(jax.random.split(first_key, clusters))
    beads = (chain_perm + jnp.arange(clusters)[:, None] * TILE).astype(jnp.int32)
    to_left = beads[:, :quarter]
    to_right = beads[:, quarter:2 * quarter]
    staying = beads[:, 2 * quarter:]
    grouped = jnp.concatenate([staying, jnp.roll(to_left, -1, axis=0), jnp.roll(to_right, 1, axis=0)], axis=1)
    shuffle = jax.vmap(lambda k: jax.random.permutation(k, TILE))(jax.random.split(second_key, clusters))
    grouped = jnp.take_along_axis(grouped, shuffle, axis=1)
    return grouped.reshape(-1).astype(jnp.int32)


def draw_near_col(key, part):
    clusters = N_BEADS // TILE
    offsets = jax.random.randint(jax.random.fold_in(key, 23), (clusters, NEARS), -2, 3)
    rows = jnp.arange(clusters, dtype=jnp.int32)[:, None]
    return jnp.mod(rows + offsets, clusters).astype(jnp.int32)


def draw_far_target(key, part):
    clusters = N_BEADS // TILE
    level_key, step_key = jax.random.split(jax.random.fold_in(key, 37))
    level = jax.random.randint(level_key, (clusters, FARS), 0, LEVELS)
    count = jnp.left_shift(jnp.full((clusters, FARS), 2, jnp.int32), level.astype(jnp.int32))
    members = clusters // count
    rows = jnp.arange(clusters, dtype=jnp.int32)[:, None]
    own = rows // members
    step = jax.random.randint(step_key, (clusters, FARS), 0, count - 1)
    target = jnp.mod(own + 1 + step, count)
    return (count - 2 + target).astype(jnp.int32)


def place_ends(result, own_key, smallest, largest):
    dims = result.shape
    spot = [jax.random.randint(jax.random.fold_in(own_key, axis), (), 0, dims[axis]) for axis in range(len(dims))]
    result = result.at[tuple(spot)].set(smallest)
    longest = dims.index(max(dims))
    spot[longest] = (spot[longest] + 1) % dims[longest]
    return result.at[tuple(spot)].set(largest)


def shard_levels(stream_key, extent, cuts, least, top_value):
    factor_of, own = 1.0, jax.random.fold_in(stream_key, 6)
    for axis_at, parts in cuts:
        steps = jnp.exp(jax.random.uniform(jax.random.fold_in(own, axis_at), (parts,), jnp.float32, least / len(cuts), top_value / len(cuts)))
        factor_of = factor_of * jnp.repeat(steps, extent[axis_at] // parts).reshape([-1 if axis == axis_at else 1 for axis in range(len(extent))])
    return factor_of


def gaussian(own_key, extent, width, reach, cuts=(), held_as=jnp.bfloat16):
    drawn = width * jax.random.normal(own_key, extent, jnp.float32)
    if cuts:
        drawn = drawn * shard_levels(own_key, extent, cuts, -0.22, 0.18)
    return jnp.clip(drawn, -reach, reach).astype(held_as)


def setup_inputs(seed: int = 0) -> dict:
    keys = jax.random.split(jax.random.key(seed), 11)
    return {
        "forces": gaussian(keys[0], (3, N_BEADS, NRHS), 1.0, 6.0, ((1, 128),)),
        "order": draw_order(jax.random.fold_in(keys[10], 71), 0),
        "bases": gaussian(keys[2], (LEVELS, RANK, 3, N_BEADS), (3 * TILE) ** -0.5, 0.21875, ((3, 128),)),
        "near_tiles": gaussian(keys[3], (N_CLU, NEARS, 3 * TILE, 3 * TILE), (3 * TILE * NEARS) ** -0.5, 0.078125, ((0, 128), (1, 4))),
        "near_col": draw_near_col(jax.random.fold_in(keys[10], 71), 0),
        "far_basis": gaussian(keys[5], (N_CLU, FARS, RANK, 3 * TILE), (FAR_DEV * RANK * N_CLU // 2) ** -0.5, 0.03125, ((0, 128), (1, 4))),
        "far_coupling": gaussian(keys[6], (N_CLU, FARS, RANK, RANK), RANK ** -0.5, 1.0, ((0, 128), (1, 4))),
        "far_scale": jnp.clip(jnp.exp(math.log(2.0) - 1.3862944 * jax.random.uniform(keys[7], (N_CLU, FARS), jnp.float32) ** shard_levels(keys[7], (N_CLU, FARS), ((0, 128), (1, 4)), -0.2, 0.2)), 0.5, 2.0),
        "far_rank": place_ends(jax.random.randint(keys[8], (N_CLU, FARS), 8, RANK + 1), jax.random.fold_in(keys[8], 1), 8, RANK).astype(jnp.int32),
        "far_target": draw_far_target(jax.random.fold_in(keys[10], 71), 0),
    }


def reference(forces, order, bases, near_tiles, near_col, far_basis, far_coupling, far_scale, far_rank, far_target):
    clusters = N_BEADS // TILE
    clustered = jnp.take(forces, order, axis=1)
    blocks = clustered.reshape(3, clusters, TILE, NRHS).transpose(1, 0, 2, 3).reshape(clusters, 3 * TILE, NRHS)
    basis_blocks = bases.reshape(LEVELS, RANK, 3, clusters, TILE).transpose(3, 0, 1, 2, 4).reshape(clusters, LEVELS * RANK, 3 * TILE)

    def piece_of(pair):
        return jnp.dot(pair[0], pair[1], preferred_element_type=jnp.float32)

    pieces = lax.map(piece_of, (basis_blocks, blocks)).reshape(clusters, LEVELS, RANK, NRHS)
    levels_list = []
    for level in range(LEVELS):
        count = 2 ** (level + 1)
        levels_list.append(pieces[:, level].reshape(count, clusters // count, RANK, NRHS).sum(axis=1))
    table = jnp.concatenate(levels_list, axis=0)

    def row(index):
        columns = near_col[index]
        total = jnp.zeros((3 * TILE, NRHS), jnp.float32)
        for slot in range(NEARS):
            total = total + jnp.dot(near_tiles[index, slot], blocks[columns[slot]], preferred_element_type=jnp.float32)
        picked = table[far_target[index]]
        keep = (jnp.arange(RANK, dtype=jnp.int32)[None, :] < far_rank[index][:, None]).astype(jnp.float32)
        masked = picked * keep[:, :, None]
        coupled = jnp.einsum("brs,bsn->brn", far_coupling[index].astype(jnp.float32), masked, precision=lax.Precision.HIGHEST)
        coupled = (coupled * far_scale[index][:, None, None]).astype(jnp.bfloat16)
        far = lax.dot_general(far_basis[index].reshape(FARS * RANK, 3 * TILE), coupled.reshape(FARS * RANK, NRHS), (((0,), (0,)), ((), ())), preferred_element_type=jnp.float32)
        return total + far

    rows = lax.map(row, jnp.arange(clusters, dtype=jnp.int32))
    return rows.reshape(clusters, 3, TILE, NRHS).transpose(1, 0, 2, 3).reshape(3, N_BEADS, NRHS)
```

```python
import functools

import jax
import jax.numpy as jnp
from jax import lax
from jax.experimental import pallas as pl
from jax.experimental.pallas import tpu as pltpu
from jax.sharding import Mesh
from jax.sharding import PartitionSpec as P

CLU = ("clu_0", "clu_1", "clu_2")
PAD = 16
F32 = jnp.float32
BF16 = jnp.bfloat16
VMEM = pl.BlockSpec(memory_space=pltpu.VMEM)
SMEM = pl.BlockSpec(memory_space=pltpu.SMEM)
ANY = pl.BlockSpec(memory_space=pl.ANY)


def params(mib):
    return pltpu.CompilerParams(vmem_limit_bytes=mib * 2**20)


def iota(shape, dim):
    return lax.broadcasted_iota(jnp.int32, shape, dim)


def dot(a, b):
    return jnp.dot(a, b, preferred_element_type=F32)


def as_column(row):
    size = row.shape[1]
    square = (size, size)
    spread = jnp.where(iota(square, 0) == iota(square, 1), jnp.broadcast_to(row, square), 0.0)
    return jnp.sum(spread, axis=1, keepdims=True)


def count_before(mask):
    size = mask.shape[1]
    square = (size, size)
    upto = (iota(square, 0) <= iota(square, 1)).astype(F32).astype(BF16)
    rows = jnp.broadcast_to(mask, (16, size)).astype(BF16)
    return dot(rows, upto)[:1] - 1.0


def chosen(column, width):
    shape = (column.shape[0], width)
    return (jnp.broadcast_to(column, shape) == iota(shape, 1).astype(F32)).astype(F32).astype(BF16)


def dress_kernel(sc, rel_ref, forces_ref, block_ref, halo_ref):
    rows, columns = forces_ref.shape
    size = rel_ref.shape[1]
    part = halo_ref.shape[1]
    start = pl.multiple_of(sc[1] * part, part)
    halo_ref[:rows] = forces_ref[:, pl.ds(start, part)]
    block_ref[:rows] = forces_ref[...]
    rel = rel_ref[...]
    high = (rel >= size).astype(jnp.int32) + (rel >= 2 * size).astype(jnp.int32)
    low = (rel - high * size).astype(F32)
    high = high.astype(F32)
    line = iota((PAD, columns), 0)
    spare = jnp.zeros((1, columns - size), F32)
    wide = [jnp.concatenate([v, spare], axis=1) for v in (low, high)]
    block_ref[rows:] = jnp.where(
        line == 0, wide[0], jnp.where(line == 1, wide[1], 0.0)
    ).astype(BF16)
    line = iota((PAD, part), 0)
    tail = jnp.zeros((PAD, part), F32)
    at = 0
    for v in (low, high):
        for i in range(size // part):
            tail = jnp.where(line == at, v[:, i * part : (i + 1) * part], tail)
            at += 1
    halo_ref[rows:] = tail.astype(BF16)


def pieces_kernel(sc, halo_ref, own_ref, pair_ref, bases_ref, keep_ref, send_ref, thin_ref):
    levels, comps, rank, size = bases_ref.shape
    rows = comps * size
    part = halo_ref.shape[1]
    quarter = size // 4
    core = sc[0]
    start = pl.multiple_of(sc[1] * part, part)
    tail = own_ref[rows:].astype(F32)
    low, high = tail[0:1, :size], tail[1:2, :size]
    seat = jnp.where(core == 0, high, 2.0 - high)
    pick = chosen(as_column(seat * size + low), 3 * size)
    sums = [jnp.zeros((rank, part), F32) for _ in range(levels)]
    for comp in range(comps):
        span = slice(comp * size, (comp + 1) * size)
        got = dot(pick[:, :size], halo_ref[span])
        got += dot(pick[:, size : 2 * size], own_ref[span, pl.ds(start, part)])
        got += dot(pick[:, 2 * size :], pair_ref[span, pl.ds(start, part)])
        got = got.astype(BF16)
        for level in range(levels):
            sums[level] += dot(bases_ref[level, comp], got)
    keep_ref[...] = jnp.where(core == 0, sums[0], sums[1])
    send_ref[...] = jnp.where(core == 0, sums[1], sums[0])
    tail = halo_ref[rows:].astype(F32)
    per = size // part
    low = jnp.concatenate([tail[i : i + 1] for i in range(per)], axis=1)
    high = jnp.concatenate([tail[per + i : per + i + 1] for i in range(per)], axis=1)
    mine = high == jnp.where(core == 0, 2.0, 0.0)
    place = count_before(mine.astype(F32))
    shape = (quarter, size)
    seats = jnp.broadcast_to(jnp.where(mine, place, -1.0), shape)
    into = (seats == iota(shape, 0).astype(F32)).astype(F32).astype(BF16)
    pack = dot(into, chosen(as_column(low), size)).astype(BF16)
    for comp in range(comps):
        thin_ref[comp] = dot(pack, own_ref[comp * size : (comp + 1) * size]).astype(BF16)


def far_kernel(slot, keeps, scale, basis_ref, coupling_ref, weights_ref, high_ref, low_ref):
    blocks, rank, _ = coupling_ref.shape
    width = high_ref.shape[1]
    lane = iota((rank, width), 1)
    for b in range(blocks):
        first = slot[b] * rank
        tile = coupling_ref[b].astype(F32) * scale[b]
        tile = jnp.concatenate([tile] * (width // rank), axis=1)
        tile = jnp.where((lane >= first) & (lane < first + keeps[b]), tile, 0.0)
        high = tile.astype(BF16)
        high_ref[b * rank : (b + 1) * rank] = high
        low_ref[b * rank : (b + 1) * rank] = (tile - high.astype(F32)).astype(BF16)
    dims = (((0,), (0,)), ((), ()))
    total = lax.dot_general(basis_ref[...], high_ref[...], dims, preferred_element_type=F32)
    total += lax.dot_general(basis_ref[...], low_ref[...], dims, preferred_element_type=F32)
    for i in range(weights_ref.shape[0]):
        weights_ref[i] = total


def near_kernel(
    sc, tiles_ref, thin, near_z, pair_far, own, pair, far_z, pair_near,
    split_ref, mine_ref, window, blocks, sems,
):
    count, rows, _ = tiles_ref.shape
    columns = own.shape[1]
    size = rows // 3
    quarter = thin.shape[1]
    groups, _, part = split_ref.shape
    core, group = sc[0], sc[1]
    seats = (thin, near_z, pair_far, own, pair, far_z, pair_near)
    for j in range(count):
        off = jnp.where(core == 0, sc[2 + j], -sc[2 + j])
        for o in range(-2, 3):

            @pl.when(off == o)
            def _(j=j, o=o):
                for w in range(3):
                    source = seats[o + 2 + w]
                    if o + w == -2:
                        for comp in range(3):
                            pltpu.make_async_copy(
                                source.at[comp],
                                window.at[j, w, pl.ds(comp * size, quarter)],
                                sems.at[j, w, comp],
                            ).start()
                            window[j, w, comp * size + quarter : (comp + 1) * size] = jnp.zeros(
                                (size - quarter, columns), BF16
                            )
                    else:
                        pltpu.make_async_copy(source, window.at[j, w], sems.at[j, w, 0]).start()

    for j in range(count):
        off = jnp.where(core == 0, sc[2 + j], -sc[2 + j])
        edge = off == -2
        for w in range(1, 3):
            pltpu.make_async_copy(own, window.at[j, w], sems.at[j, w, 0]).wait()

        @pl.when(edge)
        def _(j=j):
            for comp in range(3):
                pltpu.make_async_copy(
                    thin.at[comp], window.at[j, 0, pl.ds(comp * size, quarter)], sems.at[j, 0, comp]
                ).wait()

        @pl.when(jnp.logical_not(edge))
        def _(j=j):
            pltpu.make_async_copy(own, window.at[j, 0], sems.at[j, 0, 0]).wait()

        tail = window[j, 1, rows:].astype(F32)
        low, high = tail[0:1, :size], tail[1:2, :size]
        seat = jnp.where(core == 0, high, 2.0 - high)
        first = seat == 0.0
        place = count_before(first.astype(F32))
        low = jnp.where(jnp.logical_and(first, edge), place, low)
        pick = chosen(as_column(seat * size + low), 3 * size)
        for comp in range(3):
            span = slice(comp * size, (comp + 1) * size)
            got = dot(pick[:, :size], window[j, 0, span])
            for w in range(1, 3):
                got += dot(pick[:, w * size : (w + 1) * size], window[j, w, span])
            blocks[j, span] = got.astype(BF16)
    for r in range(3):
        span = slice(r * size, (r + 1) * size)
        total = dot(tiles_ref[0, span], blocks[0])
        for j in range(1, count):
            total += dot(tiles_ref[j, span], blocks[j])
        for i in range(groups):
            piece = total[:, i * part : (i + 1) * part]
            split_ref[i, span] = piece.astype(BF16)

            @pl.when(group == i)
            def _(piece=piece, span=span):
                mine_ref[span] = piece


def last_kernel(sc, arrived_ref, mine_ref, weights_ref, sums_ref, out_ref, table_ref):
    groups = arrived_ref.shape[0]
    count, rank, _ = sums_ref.shape
    planes = count // 2
    group, plane = sc[1], sc[2]
    half = planes // 2
    other = jnp.where(plane < half, half, 0)
    coarse = sums_ref[2 * other]
    for i in range(1, half):
        coarse += sums_ref[2 * (other + i)]
    table_ref[:rank] = coarse
    for i in range(1, planes):
        at = lax.rem(plane + i, planes)
        table_ref[i * rank : (i + 1) * rank] = sums_ref[2 * at + 1]
    weights = weights_ref[0]
    for i in range(1, groups):
        weights += weights_ref[i]
    total = mine_ref[...] + jnp.dot(
        weights, table_ref[...], precision=lax.Precision.HIGHEST, preferred_element_type=F32
    )
    for i in range(groups):
        total += jnp.where(group == i, 0.0, arrived_ref[i].astype(F32))
    out_ref[...] = total


def shape_of(dims, dtype):
    return jax.ShapeDtypeStruct(dims, dtype)


def on_device(
    forces, order, bases, near_tiles, near_col, far_basis, far_coupling, far_scale, far_rank, far_target
):
    clusters = lax.axis_size(CLU)
    planes = lax.axis_size("clu_0")
    steps = lax.axis_size("clu_1")
    groups = lax.axis_size("grp")
    own_index = lax.axis_index(CLU)
    plane = lax.axis_index("clu_0")
    core = lax.axis_index("clu_2")
    group = lax.axis_index("grp")
    size = order.shape[0]
    comps, _, columns = forces.shape
    rows = comps * size
    part = columns // groups
    levels, rank = bases.shape[:2]
    count = near_tiles.shape[1]
    far_count = far_target.shape[1]
    width = planes * rank

    def swapped(v):
        return lax.ppermute(v, "clu_2", [(0, 1), (1, 0)])

    def swapped_by(v, by):
        pairs = [(i, (i + by if i % 2 else i - by) % clusters) for i in range(clusters)]
        return lax.ppermute(v, CLU, pairs)

    def from_near(v):
        pairs = [(i, (i - 2 if i % 2 else i + 2) % clusters) for i in range(clusters)]
        return lax.ppermute(v, CLU, pairs)

    def from_far(v):
        pairs = [(i, (i + 2 if i % 2 else i - 2) % clusters) for i in range(clusters)]
        return lax.ppermute(v, CLU, pairs)

    def spread(v, axis, copies):
        many = jnp.broadcast_to(v, (copies, *v.shape))
        return lax.all_to_all(many, axis, split_axis=0, concat_axis=0, tiled=True)

    offsets = jnp.mod(near_col[0] - own_index + 2, clusters) - 2
    sc = jnp.concatenate([jnp.stack([core, group]), offsets]).astype(jnp.int32)
    rel = jnp.mod(order - (own_index - 1) * size, clusters * size).reshape(1, size)
    block, halo = pl.pallas_call(
        dress_kernel,
        out_shape=(shape_of((rows + PAD, columns), BF16), shape_of((rows + PAD, part), BF16)),
        in_specs=[SMEM, VMEM, VMEM],
        out_specs=(VMEM, VMEM),
        compiler_params=params(16),
        name="dress",
    )(sc, rel, forces.reshape(rows, columns))
    halo = swapped_by(halo, 1)
    pair = swapped(block)
    near_z = from_near(block)
    far_z = from_far(block)

    keep, send, thin = pl.pallas_call(
        pieces_kernel,
        out_shape=(
            shape_of((rank, part), F32),
            shape_of((rank, part), F32),
            shape_of((comps, size // 4, columns), BF16),
        ),
        in_specs=[SMEM, VMEM, VMEM, VMEM, VMEM],
        out_specs=(VMEM, VMEM, VMEM),
        compiler_params=params(16),
        name="pieces",
    )(sc, halo, block, pair, bases.transpose(0, 2, 1, 3))
    level_sum = keep + swapped(send)
    level_sum = jnp.sum(spread(level_sum, "clu_1", steps), axis=0)
    sums = spread(level_sum, ("clu_0", "clu_2"), planes * 2)
    thin = swapped_by(thin, 3)

    target = far_target[0]
    slot = jnp.where(target < 2, 0, jnp.mod(target - 2 - plane, planes)).astype(jnp.int32)
    weights = pl.pallas_call(
        far_kernel,
        out_shape=shape_of((groups, rows, width), F32),
        in_specs=[SMEM, SMEM, SMEM, VMEM, VMEM],
        out_specs=VMEM,
        scratch_shapes=[pltpu.VMEM((far_count * rank, width), BF16)] * 2,
        compiler_params=params(16),
        name="far_weights",
    )(slot, far_rank[0], far_scale[0], far_basis.reshape(far_count * rank, rows), far_coupling[0])
    weights = lax.all_to_all(weights, "grp", split_axis=0, concat_axis=0, tiled=True)

    pair_near = swapped(near_z)
    pair_far = swapped(far_z)
    split, mine = pl.pallas_call(
        near_kernel,
        out_shape=(shape_of((groups, rows, part), BF16), shape_of((rows, part), F32)),
        in_specs=[SMEM, VMEM] + [ANY] * 7,
        out_specs=(VMEM, VMEM),
        scratch_shapes=[
            pltpu.VMEM((count, 3, rows + PAD, columns), BF16),
            pltpu.VMEM((count, rows, columns), BF16),
            pltpu.SemaphoreType.DMA((count, 3, 3)),
        ],
        compiler_params=params(32),
        name="near",
    )(sc, near_tiles[0], thin, near_z, pair_far, block, pair, far_z, pair_near)
    arrived = lax.all_to_all(split, "grp", split_axis=0, concat_axis=0, tiled=True)
    velocity = pl.pallas_call(
        last_kernel,
        out_shape=shape_of((rows, part), F32),
        in_specs=[SMEM, VMEM, VMEM, VMEM, VMEM],
        out_specs=VMEM,
        scratch_shapes=[pltpu.VMEM((width, part), F32)],
        compiler_params=params(16),
        name="last",
    )(jnp.stack([core, group, plane]).astype(jnp.int32), arrived, mine, weights, sums)
    return velocity.reshape(comps, size, part)


def solution(mesh):
    clusters = mesh.shape["clu"]
    torus = Mesh(
        mesh.devices.reshape(mesh.shape["grp"], 4, clusters // 8, 2),
        ("grp", "clu_0", "clu_1", "clu_2"),
    )
    in_specs = (
        P(None, CLU, None),
        P(CLU),
        P(None, None, None, CLU),
        P(CLU, "grp", None, None),
        P(CLU, "grp"),
        P(CLU, "grp", None, None),
        P(CLU, "grp", None, None),
        P(CLU, "grp"),
        P(CLU, "grp"),
        P(CLU, "grp"),
    )
    return jax.shard_map(
        on_device, mesh=torus, in_specs=in_specs, out_specs=P(None, CLU, "grp"), check_vma=False
    )
```

```python
import functools

import jax
import jax.numpy as jnp
from jax import lax
from jax.experimental import pallas as pl
from jax.experimental.pallas import tpu as pltpu
from jax.sharding import Mesh
from jax.sharding import PartitionSpec as P

CLU = ("clu_0", "clu_1", "clu_2")
PAD = 16
F32 = jnp.float32
BF16 = jnp.bfloat16
VMEM = pl.BlockSpec(memory_space=pltpu.VMEM)
SMEM = pl.BlockSpec(memory_space=pltpu.SMEM)
ANY = pl.BlockSpec(memory_space=pl.ANY)
HBM = pl.BlockSpec(memory_space=pltpu.MemorySpace.HBM)


def params(mib):
    return pltpu.CompilerParams(vmem_limit_bytes=mib * 2**20)


def iota(shape, dim):
    return lax.broadcasted_iota(jnp.int32, shape, dim)


def dot(a, b):
    return jnp.dot(a, b, preferred_element_type=F32)


def as_column(row):
    size = row.shape[1]
    square = (size, size)
    spread = jnp.where(iota(square, 0) == iota(square, 1), jnp.broadcast_to(row, square), 0.0)
    return jnp.sum(spread, axis=1, keepdims=True)


def count_before(mask):
    size = mask.shape[1]
    square = (size, size)
    upto = (iota(square, 0) <= iota(square, 1)).astype(F32).astype(BF16)
    rows = jnp.broadcast_to(mask, (16, size)).astype(BF16)
    return dot(rows, upto)[:1] - 1.0


def chosen(column, width):
    shape = (column.shape[0], width)
    return (jnp.broadcast_to(column, shape) == iota(shape, 1).astype(F32)).astype(F32).astype(BF16)


def rows_of(v, width):
    return [v[:, i : i + width] for i in range(0, v.shape[1], width)]


def stacked(lines, width):
    at = iota((PAD, width), 0)
    out = jnp.zeros((PAD, width), F32)
    for i, v in enumerate(lines):
        if v.shape[1] < width:
            v = jnp.concatenate([v, jnp.zeros((1, width - v.shape[1]), F32)], axis=1)
        out = jnp.where(at == i, v, out)
    return out.astype(BF16)


def dress_kernel(clusters, sc, order_ref, forces, bases, block_ref, halo_ref, base_ref, sems):
    rows, columns = forces.shape
    comps, rank, size = base_ref.shape
    part = halo_ref.shape[1]
    start = pl.multiple_of(sc[1] * part, part)
    copies = [
        pltpu.make_async_copy(bases.at[1 - sc[0]], base_ref, sems.at[2]),
        pltpu.make_async_copy(forces.at[:, pl.ds(start, part)], halo_ref.at[pl.ds(0, rows)], sems.at[0]),
        pltpu.make_async_copy(forces, block_ref.at[pl.ds(0, rows)], sems.at[1]),
    ]
    for copy in copies:
        copy.start()
    rel = order_ref[...] - (sc[3] - 1) * size
    rel = jnp.where(rel < 0, rel + clusters * size, rel)
    rel = jnp.where(rel >= clusters * size, rel - clusters * size, rel)
    high = (rel >= size).astype(jnp.int32) + (rel >= 2 * size).astype(jnp.int32)
    low = (rel - high * size).astype(F32)
    high = high.astype(F32)
    block_ref[rows : rows + PAD] = stacked([low, high], columns)
    halo_ref[rows:] = stacked(rows_of(low, part) + rows_of(high, part), part)
    copies[0].wait()
    half = rank // 2
    for comp in range(comps):
        at = rows + PAD + comp * half
        block_ref[at : at + half, :size] = base_ref[comp, :half]
        block_ref[at : at + half, size : 2 * size] = base_ref[comp, half:]
    copies[1].wait()
    copies[2].wait()


def pieces_kernel(
    sc, order_ref, first_ref, last_ref, own_ref, pair_ref, bases_ref, after, many_ref, thin_ref, orders_ref
):
    del after
    _, comps, rank, size = bases_ref.shape
    rows = comps * size
    part = first_ref.shape[1]
    quarter = size // 4
    half = rank // 2
    per = size // part
    core = sc[0]
    start = pl.multiple_of(sc[1] * part, part)

    def narrow(ref):
        tail = ref[rows:].astype(F32)
        return [
            jnp.concatenate([tail[at + i : at + i + 1] for i in range(per)], axis=1) for at in (0, per)
        ]

    pair_tail = pair_ref[rows : rows + PAD].astype(F32)
    own_order = order_ref[...].astype(F32)
    orders = [
        narrow(first_ref),
        [own_order[0:1, :size], own_order[1:2, :size]],
        [pair_tail[0:1, :size], pair_tail[1:2, :size]],
        narrow(last_ref),
    ]
    for i, (low, high) in enumerate(orders):
        orders_ref[2 * i : 2 * i + 1] = low
        orders_ref[2 * i + 1 : 2 * i + 2] = high

    def pick_of(low, high):
        seat = jnp.where(core == 0, high, 2.0 - high)
        return chosen(as_column(seat * size + low), 3 * size)

    own_pick, pair_pick = pick_of(*orders[1]), pick_of(*orders[2])
    total = jnp.zeros((rank, part), F32)
    for comp in range(comps):
        span = slice(comp * size, (comp + 1) * size)
        line = (
            first_ref[span],
            own_ref[span, pl.ds(start, part)],
            pair_ref[span, pl.ds(start, part)],
            last_ref[span],
        )
        got = [
            sum(dot(pick[:, i * size : (i + 1) * size], line[i + at]) for i in range(3)).astype(BF16)
            for at, pick in enumerate((own_pick, pair_pick))
        ]
        at = rows + PAD + comp * half
        pair_bases = jnp.concatenate(
            [pair_ref[at : at + half, :size], pair_ref[at : at + half, size : 2 * size]], axis=0
        )
        total += dot(bases_ref[core, comp], got[0]) + dot(pair_bases, got[1])
    total = total.astype(BF16)
    for i in range(many_ref.shape[0]):
        many_ref[i] = total

    low, high = orders[0]
    mine = high == jnp.where(core == 0, 2.0, 0.0)
    place = count_before(mine.astype(F32))
    shape = (quarter, size)
    seats = jnp.broadcast_to(jnp.where(mine, place, -1.0), shape)
    into = (seats == iota(shape, 0).astype(F32)).astype(F32).astype(BF16)
    pack = dot(into, chosen(as_column(low), size)).astype(BF16)
    for comp in range(comps):
        thin_ref[comp * quarter : (comp + 1) * quarter] = dot(
            pack, own_ref[comp * size : (comp + 1) * size]
        ).astype(BF16)
    thin_ref[comps * quarter :] = stacked([low, high], thin_ref.shape[1])


def far_kernel(planes, sc, target, keeps, scale, basis_ref, coupling_ref, weights_ref, high_ref, low_ref):
    blocks, rank, _ = coupling_ref.shape
    width = high_ref.shape[1]
    lane = iota((rank, width), 1)
    for b in range(blocks):
        slot = jnp.where(target[b] < 2, 0, lax.rem(target[b] - 2 - sc[2] + planes, planes))
        first = slot * rank
        tile = coupling_ref[b].astype(F32) * scale[b]
        tile = jnp.concatenate([tile] * (width // rank), axis=1)
        tile = jnp.where((lane >= first) & (lane < first + keeps[b]), tile, 0.0)
        high = tile.astype(BF16)
        high_ref[b * rank : (b + 1) * rank] = high
        low_ref[b * rank : (b + 1) * rank] = (tile - high.astype(F32)).astype(BF16)
    dims = (((0,), (0,)), ((), ()))
    total = lax.dot_general(basis_ref[...], high_ref[...], dims, preferred_element_type=F32)
    total += lax.dot_general(basis_ref[...], low_ref[...], dims, preferred_element_type=F32)
    weights_ref[...] = total


def near_kernel(
    clusters, sc, near_col, orders_ref, tiles, own, thin, near_z, pair_far, pair, far_z, pair_near,
    split, tile_ref, thin_tail, window, blocks, result, sems, tile_sems, tail_sem, out_sems,
):
    count, rows, _ = tiles.shape
    columns = own.shape[1]
    size = rows // 3
    quarter = size // 4
    groups, _, part = split.shape
    core = sc[0]
    seats = (thin, near_z, pair_far, own, pair, far_z, pair_near)
    offs = []
    for j in range(count):
        off = near_col[j] - sc[3] + 2
        off = jnp.where(off < 0, off + clusters, off)
        off = jnp.where(off >= clusters, off - clusters, off) - 2
        offs.append(jnp.where(core == 0, off, -off))
    tail_copy = pltpu.make_async_copy(thin.at[pl.ds(3 * quarter, PAD)], thin_tail, tail_sem.at[0])
    tail_copy.start()
    for j in range(count):
        for o in range(-2, 3):

            @pl.when(offs[j] == o)
            def _(j=j, o=o):
                for w in range(3):
                    source = seats[o + 2 + w]
                    if o + w == -2:
                        for comp in range(3):
                            pltpu.make_async_copy(
                                source.at[pl.ds(comp * quarter, quarter)],
                                window.at[j, w, pl.ds(comp * size, quarter)],
                                sems.at[j, w, comp],
                            ).start()
                            window[j, w, comp * size + quarter : (comp + 1) * size] = jnp.zeros(
                                (size - quarter, columns), BF16
                            )
                    else:
                        pltpu.make_async_copy(
                            source.at[pl.ds(0, rows)], window.at[j, w], sems.at[j, w, 0]
                        ).start()

        pltpu.make_async_copy(tiles.at[j], tile_ref.at[j], tile_sems.at[j]).start()
    tail_copy.wait()
    tail = thin_tail[...].astype(F32)
    for j in range(count):
        edge = offs[j] == -2
        low, high = tail[0:1, :size], tail[1:2, :size]
        for i in range(4):
            low = jnp.where(offs[j] == i - 1, orders_ref[2 * i : 2 * i + 1], low)
            high = jnp.where(offs[j] == i - 1, orders_ref[2 * i + 1 : 2 * i + 2], high)
        seat = jnp.where(core == 0, high, 2.0 - high)
        first = seat == 0.0
        place = count_before(first.astype(F32))
        low = jnp.where(jnp.logical_and(first, edge), place, low)
        pick = chosen(as_column(seat * size + low), 3 * size)
        for w in range(1, 3):
            pltpu.make_async_copy(own, window.at[j, w], sems.at[j, w, 0]).wait()

        @pl.when(edge)
        def _(j=j):
            for comp in range(3):
                pltpu.make_async_copy(
                    thin.at[pl.ds(comp * quarter, quarter)],
                    window.at[j, 0, pl.ds(comp * size, quarter)],
                    sems.at[j, 0, comp],
                ).wait()

        @pl.when(jnp.logical_not(edge))
        def _(j=j):
            pltpu.make_async_copy(own, window.at[j, 0], sems.at[j, 0, 0]).wait()

        for comp in range(3):
            span = slice(comp * size, (comp + 1) * size)
            got = dot(pick[:, :size], window[j, 0, span])
            for w in range(1, 3):
                got += dot(pick[:, w * size : (w + 1) * size], window[j, w, span])
            blocks[j, span] = got.astype(BF16)
    for j in range(count):
        pltpu.make_async_copy(tiles.at[j], tile_ref.at[j], tile_sems.at[j]).wait()
    outs = []
    for r in range(3):
        span = slice(r * size, (r + 1) * size)
        total = dot(tile_ref[0, span], blocks[0])
        for j in range(1, count):
            total += dot(tile_ref[j, span], blocks[j])
        for i in range(groups):
            result[i, span] = total[:, i * part : (i + 1) * part].astype(BF16)
        outs.append(
            pltpu.make_async_copy(
                result.at[:, pl.ds(r * size, size)], split.at[:, pl.ds(r * size, size)], out_sems.at[r]
            )
        )
        outs[-1].start()
    for copy in outs:
        copy.wait()


def add_kernel(a_ref, b_ref, out_ref):
    out_ref[...] = a_ref[...] + b_ref[...]


def reduce_kernel(many_ref, sums_ref):
    total = many_ref[0].astype(F32)
    for i in range(1, many_ref.shape[0]):
        total += many_ref[i].astype(F32)
    for i in range(sums_ref.shape[0]):
        sums_ref[i] = total


def last_kernel(sc, arrived_ref, sums_ref, *refs):
    *weights_refs, out_ref, table_ref = refs
    groups = arrived_ref.shape[0]
    count, rank, _ = sums_ref.shape
    planes = count // 2
    plane = sc[2]
    half = planes // 2
    other = jnp.where(plane < half, half, 0)
    coarse = sums_ref[2 * other]
    for i in range(1, half):
        coarse += sums_ref[2 * (other + i)]
    table_ref[:rank] = coarse
    for i in range(1, planes):
        at = lax.rem(plane + i, planes)
        table_ref[i * rank : (i + 1) * rank] = sums_ref[2 * at + 1]
    weights = weights_refs[0][...]
    for ref in weights_refs[1:]:
        weights += ref[...]
    total = jnp.dot(
        weights, table_ref[...], precision=lax.Precision.HIGHEST, preferred_element_type=F32
    )
    for i in range(groups):
        total += arrived_ref[i].astype(F32)
    out_ref[...] = total


def tie_kernel(*refs):
    del refs


def tied(value, *after):
    return pl.pallas_call(
        tie_kernel,
        out_shape=shape_of(value.shape, value.dtype),
        in_specs=[ANY] * (1 + len(after)),
        out_specs=ANY,
        input_output_aliases={0: 0},
        compiler_params=params(1),
        name="tie",
    )(value, *after)


def in_hbm(*values):
    return [pltpu.with_memory_space_constraint(v, pltpu.MemorySpace.HBM) for v in values]


def shape_of(dims, dtype):
    return jax.ShapeDtypeStruct(dims, dtype)


def on_device(
    forces, order, bases, near_tiles, near_col, far_basis, far_coupling, far_scale, far_rank, far_target
):
    clusters = lax.axis_size(CLU)
    planes = lax.axis_size("clu_0")
    steps = lax.axis_size("clu_1")
    groups = lax.axis_size("grp")
    size = order.shape[0]
    comps, _, columns = forces.shape
    rows = comps * size
    part = columns // groups
    _, rank = bases.shape[:2]
    count = near_tiles.shape[1]
    far_count = far_target.shape[1]
    width = planes * rank
    sc = jnp.stack(
        [lax.axis_index("clu_2"), lax.axis_index("grp"), lax.axis_index("clu_0"), lax.axis_index(CLU)]
    ).astype(jnp.int32)

    def swapped(v):
        return lax.ppermute(v, "clu_2", [(0, 1), (1, 0)])

    def sent(v, by):
        pairs = [(i, (i + by if i % 2 else i - by) % clusters) for i in range(clusters)]
        return lax.ppermute(v, CLU, pairs)

    def exchanged(v, axis):
        return lax.all_to_all(v, axis, split_axis=0, concat_axis=0, tiled=True)

    chain = forces.reshape(rows, columns)
    near_z = sent(chain, -2)
    far_z = sent(chain, 2)
    by_comp = bases.transpose(0, 2, 1, 3)
    block, halo = pl.pallas_call(
        functools.partial(dress_kernel, clusters),
        out_shape=(
            shape_of((rows + PAD + comps * rank // 2, columns), BF16),
            shape_of((rows + PAD, part), BF16),
        ),
        in_specs=[SMEM, VMEM, HBM, HBM],
        out_specs=(VMEM, VMEM),
        scratch_shapes=[pltpu.VMEM((comps, rank, size), BF16), pltpu.SemaphoreType.DMA((3,))],
        compiler_params=params(8),
        name="dress",
    )(sc, order.reshape(1, size), *in_hbm(chain, by_comp))
    first = sent(halo, 1)
    last = sent(halo, 2)
    pair = swapped(block)
    weights = pl.pallas_call(
        functools.partial(far_kernel, planes),
        out_shape=shape_of((rows, width), F32),
        in_specs=[SMEM, SMEM, SMEM, SMEM, VMEM, VMEM],
        out_specs=VMEM,
        scratch_shapes=[pltpu.VMEM((far_count * rank, width), BF16)] * 2,
        compiler_params=params(8),
        name="far_weights",
    )(
        sc, far_target[0], far_rank[0], far_scale[0],
        far_basis.reshape(far_count * rank, rows), far_coupling[0],
    )
    other = lax.ppermute(weights, "grp", [(i, i ^ 1) for i in range(groups)])
    both = pl.pallas_call(
        add_kernel,
        out_shape=shape_of((rows, width), F32),
        in_specs=[VMEM, VMEM],
        out_specs=VMEM,
        compiler_params=params(4),
        name="add",
    )(weights, other)
    rest = lax.ppermute(both, "grp", [(i, groups - 1 - i) for i in range(groups)])

    many, thin, orders = pl.pallas_call(
        pieces_kernel,
        out_shape=(
            shape_of((steps, rank, part), BF16),
            shape_of((rows // 4 + PAD, columns), BF16),
            shape_of((8, size), F32),
        ),
        in_specs=[SMEM] + [VMEM] * 6 + [ANY],
        out_specs=(VMEM, VMEM, VMEM),
        compiler_params=params(12),
        name="pieces",
    )(sc, block[rows : rows + PAD], first, last, chain, pair, by_comp, weights)
    many = exchanged(many, "clu_1")
    thin = sent(thin, 3)

    near_z = tied(near_z, many, thin)
    far_z = tied(far_z, many, both)
    pair_near = swapped(near_z)
    pair_far = swapped(far_z)
    sums = pl.pallas_call(
        reduce_kernel,
        out_shape=shape_of((2 * planes, rank, part), F32),
        in_specs=[VMEM],
        out_specs=VMEM,
        compiler_params=params(4),
        name="reduce",
    )(many)
    sums = exchanged(sums, ("clu_0", "clu_2"))
    split = pl.pallas_call(
        functools.partial(near_kernel, clusters),
        out_shape=shape_of((groups, rows, part), BF16),
        in_specs=[SMEM, SMEM, VMEM, HBM, HBM] + [ANY] * 6,
        out_specs=HBM,
        scratch_shapes=[
            pltpu.VMEM((count, rows, rows), BF16),
            pltpu.VMEM((PAD, columns), BF16),
            pltpu.VMEM((count, 3, rows, columns), BF16),
            pltpu.VMEM((count, rows, columns), BF16),
            pltpu.VMEM((groups, rows, part), BF16),
            pltpu.SemaphoreType.DMA((count, 3, 3)),
            pltpu.SemaphoreType.DMA((count,)),
            pltpu.SemaphoreType.DMA((1,)),
            pltpu.SemaphoreType.DMA((3,)),
        ],
        compiler_params=params(20),
        name="near",
    )(
        sc, near_col[0], orders,
        *in_hbm(near_tiles[0], chain), thin, near_z, pair_far, pair, far_z, pair_near,
    )
    arrived = exchanged(tied(split, rest), "grp")
    velocity = pl.pallas_call(
        last_kernel,
        out_shape=shape_of((rows, part), F32),
        in_specs=[SMEM, VMEM, VMEM] + [VMEM] * 2,
        out_specs=VMEM,
        scratch_shapes=[pltpu.VMEM((width, part), F32)],
        compiler_params=params(8),
        name="last",
    )(sc, arrived, sums, both, rest)
    return velocity.reshape(comps, size, part)


def solution(mesh):
    clusters = mesh.shape["clu"]
    torus = Mesh(
        mesh.devices.reshape(mesh.shape["grp"], 4, clusters // 8, 2),
        ("grp", "clu_0", "clu_1", "clu_2"),
    )
    in_specs = (
        P(None, CLU, None),
        P(CLU),
        P(None, None, None, CLU),
        P(CLU, "grp", None, None),
        P(CLU, "grp"),
        P(CLU, "grp", None, None),
        P(CLU, "grp", None, None),
        P(CLU, "grp"),
        P(CLU, "grp"),
        P(CLU, "grp"),
    )
    return jax.shard_map(
        on_device, mesh=torus, in_specs=in_specs, out_specs=P(None, CLU, "grp"), check_vma=False
    )
```

```python
import functools

import jax
import jax.numpy as jnp
from jax import lax
from jax.experimental import pallas as pl
from jax.experimental.pallas import tpu as pltpu
from jax.sharding import Mesh
from jax.sharding import PartitionSpec as P

CLU = ("clu_0", "clu_1", "clu_2")
PAD = 16
F32 = jnp.float32
BF16 = jnp.bfloat16
VMEM = pl.BlockSpec(memory_space=pltpu.VMEM)
SMEM = pl.BlockSpec(memory_space=pltpu.SMEM)
ANY = pl.BlockSpec(memory_space=pl.ANY)
HBM = pl.BlockSpec(memory_space=pltpu.MemorySpace.HBM)


def params(mib):
    return pltpu.CompilerParams(vmem_limit_bytes=mib * 2**20)


def iota(shape, dim):
    return lax.broadcasted_iota(jnp.int32, shape, dim)


def dot(a, b):
    return jnp.dot(a, b, preferred_element_type=F32)


def as_column(row):
    size = row.shape[1]
    square = (size, size)
    spread = jnp.where(iota(square, 0) == iota(square, 1), jnp.broadcast_to(row, square), 0.0)
    return jnp.sum(spread, axis=1, keepdims=True)


def count_before(mask):
    size = mask.shape[1]
    square = (size, size)
    upto = (iota(square, 0) <= iota(square, 1)).astype(F32).astype(BF16)
    rows = jnp.broadcast_to(mask, (16, size)).astype(BF16)
    return dot(rows, upto)[:1] - 1.0


def chosen(column, width):
    shape = (column.shape[0], width)
    return (jnp.broadcast_to(column, shape) == iota(shape, 1).astype(F32)).astype(F32).astype(BF16)


def rows_of(v, width):
    return [v[:, i : i + width] for i in range(0, v.shape[1], width)]


def stacked(lines, width):
    at = iota((PAD, width), 0)
    out = jnp.zeros((PAD, width), F32)
    for i, v in enumerate(lines):
        if v.shape[1] < width:
            v = jnp.concatenate([v, jnp.zeros((1, width - v.shape[1]), F32)], axis=1)
        out = jnp.where(at == i, v, out)
    return out.astype(BF16)


def halo_kernel(clusters, sc, order, forces, halo_ref, lines_ref, order_ref, sems):
    rows, columns = forces.shape
    size = order.shape[1]
    part = halo_ref.shape[1]
    start = pl.multiple_of(sc[1] * part, part)
    copies = [
        pltpu.make_async_copy(order, order_ref, sems.at[0]),
        pltpu.make_async_copy(forces.at[:, pl.ds(start, part)], halo_ref.at[pl.ds(0, rows)], sems.at[1]),
    ]
    for copy in copies:
        copy.start()
    copies[0].wait()
    rel = order_ref[...] - (sc[3] - 1) * size
    rel = jnp.where(rel < 0, rel + clusters * size, rel)
    rel = jnp.where(rel >= clusters * size, rel - clusters * size, rel)
    high = (rel >= size).astype(jnp.int32) + (rel >= 2 * size).astype(jnp.int32)
    low = (rel - high * size).astype(F32)
    high = high.astype(F32)
    lines_ref[...] = stacked([low, high], columns)
    halo_ref[rows:] = stacked(rows_of(low, part) + rows_of(high, part), part)
    copies[1].wait()


def block_kernel(lines_ref, forces, block, sems):
    rows = forces.shape[0]
    copies = [
        pltpu.make_async_copy(forces, block.at[pl.ds(0, rows)], sems.at[0]),
        pltpu.make_async_copy(lines_ref, block.at[pl.ds(rows, PAD)], sems.at[1]),
    ]
    for copy in copies:
        copy.start()
    for copy in copies:
        copy.wait()


def pieces_kernel(sc, halo_ref, own_ref, pair_ref, bases_ref, keep_ref, send_ref, thin, thin_ref, sem):
    levels, comps, rank, size = bases_ref.shape
    rows = comps * size
    part = halo_ref.shape[1]
    quarter = size // 4
    core = sc[0]
    start = pl.multiple_of(sc[1] * part, part)
    tail = own_ref[rows:].astype(F32)
    low, high = tail[0:1, :size], tail[1:2, :size]
    seat = jnp.where(core == 0, high, 2.0 - high)
    pick = chosen(as_column(seat * size + low), 3 * size)
    sums = [jnp.zeros((rank, part), F32) for _ in range(levels)]
    for comp in range(comps):
        span = slice(comp * size, (comp + 1) * size)
        got = dot(pick[:, :size], halo_ref[span])
        got += dot(pick[:, size : 2 * size], own_ref[span, pl.ds(start, part)])
        got += dot(pick[:, 2 * size :], pair_ref[span, pl.ds(start, part)])
        got = got.astype(BF16)
        for level in range(levels):
            sums[level] += dot(bases_ref[level, comp], got)
    keep_ref[...] = jnp.where(core == 0, sums[0], sums[1])
    send_ref[...] = jnp.where(core == 0, sums[1], sums[0])
    tail = halo_ref[rows:].astype(F32)
    per = size // part
    low = jnp.concatenate([tail[i : i + 1] for i in range(per)], axis=1)
    high = jnp.concatenate([tail[per + i : per + i + 1] for i in range(per)], axis=1)
    mine = high == jnp.where(core == 0, 2.0, 0.0)
    place = count_before(mine.astype(F32))
    shape = (quarter, size)
    seats = jnp.broadcast_to(jnp.where(mine, place, -1.0), shape)
    into = (seats == iota(shape, 0).astype(F32)).astype(F32).astype(BF16)
    pack = dot(into, chosen(as_column(low), size)).astype(BF16)
    for comp in range(comps):
        thin_ref[comp] = dot(pack, own_ref[comp * size : (comp + 1) * size]).astype(BF16)
    copy = pltpu.make_async_copy(thin_ref, thin, sem.at[0])
    copy.start()
    copy.wait()


def near_kernel(
    clusters, planes, sc, near_col, target, keeps, scale, coupling, tiles,
    own, thin, near_z, pair_far, pair, far_z, pair_near,
    total_ref, high_ref, low_ref,
    col_ref, target_ref, keep_ref, scale_ref, coupling_ref, tile_ref, window, blocks,
    sems, tile_sems, small_sems,
):
    count, rows, _ = tiles.shape
    columns = own.shape[1]
    size = rows // 3
    quarter = size // 4
    core = sc[0]
    pairs = (
        (near_col, col_ref), (target, target_ref), (keeps, keep_ref), (scale, scale_ref),
        (coupling, coupling_ref),
    )
    smalls = [pltpu.make_async_copy(a, b, small_sems.at[i]) for i, (a, b) in enumerate(pairs)]
    for copy in smalls:
        copy.start()
    seats = (thin, near_z, pair_far, own, pair, far_z, pair_near)
    for j in range(count):
        pltpu.make_async_copy(tiles.at[j], tile_ref.at[j], tile_sems.at[j]).start()
    smalls[0].wait()
    offs = []
    for j in range(count):
        off = col_ref[0, j] - sc[3] + 2
        off = jnp.where(off < 0, off + clusters, off)
        off = jnp.where(off >= clusters, off - clusters, off) - 2
        offs.append(jnp.where(core == 0, off, -off))
    for j in range(count):
        for o in range(-2, 3):

            @pl.when(offs[j] == o)
            def _(j=j, o=o):
                for w in range(3):
                    source = seats[o + 2 + w]
                    if o + w == -2:
                        for comp in range(3):
                            pltpu.make_async_copy(
                                source.at[comp],
                                window.at[j, w, pl.ds(comp * size, quarter)],
                                sems.at[j, w, comp],
                            ).start()
                            window[j, w, comp * size + quarter : (comp + 1) * size] = jnp.zeros(
                                (size - quarter, columns), BF16
                            )
                    else:
                        pltpu.make_async_copy(source, window.at[j, w], sems.at[j, w, 0]).start()

    for copy in smalls[1:]:
        copy.wait()
    far_count, rank, _ = coupling_ref.shape
    width = high_ref.shape[1]
    lane = iota((rank, width), 1)
    for b in range(far_count):
        goal = target_ref[0, b]
        start = jnp.where(goal < 2, 0, lax.rem(goal - 2 - sc[2] + planes, planes)) * rank
        tile = coupling_ref[b].astype(F32) * scale_ref[0, b]
        tile = jnp.concatenate([tile] * (width // rank), axis=1)
        tile = jnp.where((lane >= start) & (lane < start + keep_ref[0, b]), tile, 0.0)
        high = tile.astype(BF16)
        high_ref[b * rank : (b + 1) * rank] = high
        low_ref[b * rank : (b + 1) * rank] = (tile - high.astype(F32)).astype(BF16)

    for j in range(count):
        edge = offs[j] == -2
        for w in range(1, 3):
            pltpu.make_async_copy(own, window.at[j, w], sems.at[j, w, 0]).wait()

        @pl.when(edge)
        def _(j=j):
            for comp in range(3):
                pltpu.make_async_copy(
                    thin.at[comp], window.at[j, 0, pl.ds(comp * size, quarter)], sems.at[j, 0, comp]
                ).wait()

        @pl.when(jnp.logical_not(edge))
        def _(j=j):
            pltpu.make_async_copy(own, window.at[j, 0], sems.at[j, 0, 0]).wait()

        tail = window[j, 1, rows:].astype(F32)
        low, high = tail[0:1, :size], tail[1:2, :size]
        seat = jnp.where(core == 0, high, 2.0 - high)
        first = seat == 0.0
        place = count_before(first.astype(F32))
        low = jnp.where(jnp.logical_and(first, edge), place, low)
        pick = chosen(as_column(seat * size + low), 3 * size)
        for comp in range(3):
            span = slice(comp * size, (comp + 1) * size)
            got = dot(pick[:, :size], window[j, 0, span])
            for w in range(1, 3):
                got += dot(pick[:, w * size : (w + 1) * size], window[j, w, span])
            blocks[j, span] = got.astype(BF16)
    for j in range(count):
        pltpu.make_async_copy(tiles.at[j], tile_ref.at[j], tile_sems.at[j]).wait()
    for r in range(3):
        span = slice(r * size, (r + 1) * size)
        total = dot(tile_ref[0, span], blocks[0])
        for j in range(1, count):
            total += dot(tile_ref[j, span], blocks[j])
        total_ref[span] = total


def reduce_kernel(many_ref, sums, sums_ref, sem):
    total = many_ref[0]
    for i in range(1, many_ref.shape[0]):
        total += many_ref[i]
    for i in range(sums_ref.shape[0]):
        sums_ref[i] = total
    copy = pltpu.make_async_copy(sums_ref, sums, sem.at[0])
    copy.start()
    copy.wait()


def mix_kernel(
    planes, sc, near, sums, basis, high_ref, low_ref, split,
    near_ref, sums_ref, basis_ref, table_ref, coupled_ref, result, in_sems, sems,
):
    pairs = ((sums, sums_ref), (basis, basis_ref), (near, near_ref))
    copies = [pltpu.make_async_copy(a, b, in_sems.at[i]) for i, (a, b) in enumerate(pairs)]
    for copy in copies:
        copy.start()
    copies[0].wait()
    groups, rows, part = split.shape
    rank = sums_ref.shape[1]
    plane = sc[2]
    half = planes // 2
    other = jnp.where(plane < half, half, 0)
    for y in range(groups):
        lanes = slice(y * part, (y + 1) * part)
        base = y * 2 * planes
        coarse = sums_ref[base + 2 * other]
        for i in range(1, half):
            coarse += sums_ref[base + 2 * (other + i)]
        table_ref[:rank, lanes] = coarse
        for i in range(1, planes):
            at = lax.rem(plane + i, planes)
            table_ref[i * rank : (i + 1) * rank, lanes] = sums_ref[base + 2 * at + 1]
    table = table_ref[...]
    high = table.astype(BF16)
    low = (table - high.astype(F32)).astype(BF16)
    step = high_ref.shape[0] // 2
    for i in range(2):
        span = slice(i * step, (i + 1) * step)
        coupled = dot(high_ref[span], high) + dot(high_ref[span], low) + dot(low_ref[span], high)
        coupled_ref[span] = coupled.astype(BF16)
    copies[1].wait()
    copies[2].wait()
    outs = []
    size = rows // 3
    for r in range(3):
        span = slice(r * size, (r + 1) * size)
        total = near_ref[span] + lax.dot_general(
            basis_ref[:, span], coupled_ref[...], (((0,), (0,)), ((), ())), preferred_element_type=F32
        )
        for i in range(groups):
            result[i, span] = total[:, i * part : (i + 1) * part].astype(BF16)
        here = pl.ds(r * size, size)
        outs.append(pltpu.make_async_copy(result.at[:, here], split.at[:, here], sems.at[r]))
        outs[-1].start()
    for copy in outs:
        copy.wait()


def last_kernel(arrived_ref, out_ref):
    total = arrived_ref[0].astype(F32)
    for i in range(1, arrived_ref.shape[0]):
        total += arrived_ref[i].astype(F32)
    out_ref[...] = total


def tie_kernel(*refs):
    del refs


def tied(value, *after):
    return pl.pallas_call(
        tie_kernel,
        out_shape=shape_of(value.shape, value.dtype),
        in_specs=[ANY] * (1 + len(after)),
        out_specs=ANY,
        input_output_aliases={0: 0},
        compiler_params=params(1),
        name="tie",
    )(value, *after)


def in_hbm(*values):
    return [pltpu.with_memory_space_constraint(v, pltpu.MemorySpace.HBM) for v in values]


def shape_of(dims, dtype):
    return jax.ShapeDtypeStruct(dims, dtype)


def on_device(
    forces, order, bases, near_tiles, near_col, far_basis, far_coupling, far_scale, far_rank, far_target
):
    clusters = lax.axis_size(CLU)
    planes = lax.axis_size("clu_0")
    steps = lax.axis_size("clu_1")
    groups = lax.axis_size("grp")
    size = order.shape[0]
    comps, _, columns = forces.shape
    rows = comps * size
    part = columns // groups
    _, rank = bases.shape[:2]
    count = near_tiles.shape[1]
    far_count = far_target.shape[1]
    width = planes * rank
    sc = jnp.stack(
        [lax.axis_index("clu_2"), lax.axis_index("grp"), lax.axis_index("clu_0"), lax.axis_index(CLU)]
    ).astype(jnp.int32)

    def swapped(v):
        return lax.ppermute(v, "clu_2", [(0, 1), (1, 0)])

    def sent(v, by):
        pairs = [(i, (i + by if i % 2 else i - by) % clusters) for i in range(clusters)]
        return lax.ppermute(v, CLU, pairs)

    def exchanged(v, axis):
        return lax.all_to_all(v, axis, split_axis=0, concat_axis=0, tiled=True)

    chain = forces.reshape(rows, columns)
    halo, lines = pl.pallas_call(
        functools.partial(halo_kernel, clusters),
        out_shape=(shape_of((rows + PAD, part), BF16), shape_of((PAD, columns), BF16)),
        in_specs=[SMEM, HBM, HBM],
        out_specs=(VMEM, VMEM),
        scratch_shapes=[pltpu.VMEM((1, size), jnp.int32), pltpu.SemaphoreType.DMA((2,))],
        compiler_params=params(4),
        name="halo",
    )(sc, *in_hbm(order.reshape(1, size), chain))
    halo = sent(halo, 1)
    block = pl.pallas_call(
        block_kernel,
        out_shape=shape_of((rows + PAD, columns), BF16),
        in_specs=[VMEM, HBM],
        out_specs=HBM,
        scratch_shapes=[pltpu.SemaphoreType.DMA((2,))],
        compiler_params=params(4),
        name="block",
    )(lines, *in_hbm(chain))
    pair = swapped(block)
    near_z = sent(block, -2)
    far_z = sent(block, 2)

    keep, send, thin = pl.pallas_call(
        pieces_kernel,
        out_shape=(
            shape_of((rank, part), F32),
            shape_of((rank, part), F32),
            shape_of((comps, size // 4, columns), BF16),
        ),
        in_specs=[SMEM, VMEM, VMEM, VMEM, VMEM],
        out_specs=(VMEM, VMEM, HBM),
        scratch_shapes=[
            pltpu.VMEM((comps, size // 4, columns), BF16),
            pltpu.SemaphoreType.DMA((1,)),
        ],
        compiler_params=params(12),
        name="pieces",
    )(sc, halo, block, pair, bases.transpose(0, 2, 1, 3))
    level_sum = keep + swapped(send)
    many = exchanged(jnp.broadcast_to(level_sum, (steps, rank, part)), "clu_1")
    thin = sent(thin, 3)
    many = tied(many, near_z, far_z, *in_hbm(thin))
    pair_near = swapped(near_z)
    pair_far = swapped(far_z)
    fan = groups * 2 * planes
    sums = pl.pallas_call(
        reduce_kernel,
        out_shape=shape_of((fan, rank, part), F32),
        in_specs=[VMEM],
        out_specs=HBM,
        scratch_shapes=[pltpu.VMEM((fan, rank, part), F32), pltpu.SemaphoreType.DMA((1,))],
        compiler_params=params(58),
        name="reduce",
    )(many)
    sums = exchanged(sums, ("grp", "clu_0", "clu_2"))
    near, high, low = pl.pallas_call(
        functools.partial(near_kernel, clusters, planes),
        out_shape=(shape_of((rows, columns), F32),) + (shape_of((far_count * rank, width), BF16),) * 2,
        in_specs=[SMEM] + [HBM] * 6 + [ANY] * 7,
        out_specs=(VMEM, VMEM, VMEM),
        scratch_shapes=[
            pltpu.SMEM((1, count), jnp.int32),
            pltpu.SMEM((1, far_count), jnp.int32),
            pltpu.SMEM((1, far_count), jnp.int32),
            pltpu.SMEM((1, far_count), F32),
            pltpu.VMEM((far_count, rank, rank), BF16),
            pltpu.VMEM((count, rows, rows), BF16),
            pltpu.VMEM((count, 3, rows + PAD, columns), BF16),
            pltpu.VMEM((count, rows, columns), BF16),
            pltpu.SemaphoreType.DMA((count, 3, 3)),
            pltpu.SemaphoreType.DMA((count,)),
            pltpu.SemaphoreType.DMA((5,)),
        ],
        compiler_params=params(48),
        name="near",
    )(
        sc, *in_hbm(near_col, far_target, far_rank, far_scale, far_coupling[0], near_tiles[0]),
        block, *in_hbm(thin), near_z, pair_far, pair, far_z, pair_near,
    )
    split = pl.pallas_call(
        functools.partial(mix_kernel, planes),
        out_shape=shape_of((groups, rows, part), BF16),
        in_specs=[SMEM, HBM, HBM, HBM, VMEM, VMEM],
        out_specs=HBM,
        scratch_shapes=[
            pltpu.VMEM((rows, columns), F32),
            pltpu.VMEM((fan, rank, part), F32),
            pltpu.VMEM((far_count * rank, rows), BF16),
            pltpu.VMEM((width, columns), F32),
            pltpu.VMEM((far_count * rank, columns), BF16),
            pltpu.VMEM((groups, rows, part), BF16),
            pltpu.SemaphoreType.DMA((3,)),
            pltpu.SemaphoreType.DMA((3,)),
        ],
        compiler_params=params(16),
        name="mix",
    )(sc, *in_hbm(near, sums, far_basis.reshape(far_count * rank, rows)), high, low)
    arrived = exchanged(split, "grp")
    velocity = pl.pallas_call(
        last_kernel,
        out_shape=shape_of((rows, part), F32),
        in_specs=[VMEM],
        out_specs=VMEM,
        compiler_params=params(4),
        name="last",
    )(arrived)
    return velocity.reshape(comps, size, part)


def solution(mesh):
    clusters = mesh.shape["clu"]
    torus = Mesh(
        mesh.devices.reshape(mesh.shape["grp"], 4, clusters // 8, 2),
        ("grp", "clu_0", "clu_1", "clu_2"),
    )
    in_specs = (
        P(None, CLU, None),
        P(CLU),
        P(None, None, None, CLU),
        P(CLU, "grp", None, None),
        P(CLU, "grp"),
        P(CLU, "grp", None, None),
        P(CLU, "grp", None, None),
        P(CLU, "grp"),
        P(CLU, "grp"),
        P(CLU, "grp"),
    )
    return jax.shard_map(
        on_device, mesh=torus, in_specs=in_specs, out_specs=P(None, CLU, "grp"), check_vma=False
    )
```

```python
import functools

import jax
import jax.numpy as jnp
from jax import lax
from jax.experimental import pallas as pl
from jax.experimental.pallas import tpu as pltpu
from jax.sharding import Mesh
from jax.sharding import PartitionSpec as P

CLU = ("clu_0", "clu_1", "clu_2")
PAD = 16
F32 = jnp.float32
BF16 = jnp.bfloat16
VMEM = pl.BlockSpec(memory_space=pltpu.VMEM)
SMEM = pl.BlockSpec(memory_space=pltpu.SMEM)
ANY = pl.BlockSpec(memory_space=pl.ANY)
HBM = pl.BlockSpec(memory_space=pltpu.MemorySpace.HBM)


def params(mib):
    return pltpu.CompilerParams(vmem_limit_bytes=mib * 2**20)


def iota(shape, dim):
    return lax.broadcasted_iota(jnp.int32, shape, dim)


def dot(a, b):
    return jnp.dot(a, b, preferred_element_type=F32)


def as_column(row):
    size = row.shape[1]
    square = (size, size)
    spread = jnp.where(iota(square, 0) == iota(square, 1), jnp.broadcast_to(row, square), 0.0)
    return jnp.sum(spread, axis=1, keepdims=True)


def count_before(mask):
    size = mask.shape[1]
    square = (size, size)
    upto = (iota(square, 0) <= iota(square, 1)).astype(F32).astype(BF16)
    rows = jnp.broadcast_to(mask, (16, size)).astype(BF16)
    return dot(rows, upto)[:1] - 1.0


def chosen(column, width):
    shape = (column.shape[0], width)
    return (jnp.broadcast_to(column, shape) == iota(shape, 1).astype(F32)).astype(F32).astype(BF16)


def rows_of(v, width):
    return [v[:, i : i + width] for i in range(0, v.shape[1], width)]


def stacked(lines, width):
    at = iota((PAD, width), 0)
    out = jnp.zeros((PAD, width), F32)
    for i, v in enumerate(lines):
        if v.shape[1] < width:
            v = jnp.concatenate([v, jnp.zeros((1, width - v.shape[1]), F32)], axis=1)
        out = jnp.where(at == i, v, out)
    return out.astype(BF16)


def dress_kernel(clusters, sc, order, forces, halo_ref, block, order_ref, lines_ref, sems):
    rows, columns = forces.shape
    size = order.shape[1]
    part = halo_ref.shape[1]
    start = pl.multiple_of(sc[1] * part, part)
    copies = [
        pltpu.make_async_copy(order, order_ref, sems.at[0]),
        pltpu.make_async_copy(forces.at[:, pl.ds(start, part)], halo_ref.at[pl.ds(0, rows)], sems.at[1]),
        pltpu.make_async_copy(forces, block.at[pl.ds(0, rows)], sems.at[2]),
    ]
    for copy in copies:
        copy.start()
    copies[0].wait()
    rel = order_ref[...] - (sc[3] - 1) * size
    rel = jnp.where(rel < 0, rel + clusters * size, rel)
    rel = jnp.where(rel >= clusters * size, rel - clusters * size, rel)
    high = (rel >= size).astype(jnp.int32) + (rel >= 2 * size).astype(jnp.int32)
    low = (rel - high * size).astype(F32)
    high = high.astype(F32)
    lines_ref[...] = stacked([low, high], columns)
    copy = pltpu.make_async_copy(lines_ref, block.at[pl.ds(rows, PAD)], sems.at[3])
    copy.start()
    halo_ref[rows:] = stacked(rows_of(low, part) + rows_of(high, part), part)
    copy.wait()
    copies[1].wait()
    copies[2].wait()


def pieces_kernel(sc, halo_ref, own_ref, pair_ref, bases_ref, keep_ref, send_ref):
    levels, comps, rank, size = bases_ref.shape
    rows = comps * size
    part = halo_ref.shape[1]
    core = sc[0]
    start = pl.multiple_of(sc[1] * part, part)
    tail = own_ref[rows:].astype(F32)
    low, high = tail[0:1, :size], tail[1:2, :size]
    seat = jnp.where(core == 0, high, 2.0 - high)
    pick = chosen(as_column(seat * size + low), 3 * size)
    sums = [jnp.zeros((rank, part), F32) for _ in range(levels)]
    for comp in range(comps):
        span = slice(comp * size, (comp + 1) * size)
        got = dot(pick[:, :size], halo_ref[span])
        got += dot(pick[:, size : 2 * size], own_ref[span, pl.ds(start, part)])
        got += dot(pick[:, 2 * size :], pair_ref[span, pl.ds(start, part)])
        got = got.astype(BF16)
        for level in range(levels):
            sums[level] += dot(bases_ref[level, comp], got)
    keep_ref[...] = jnp.where(core == 0, sums[0], sums[1])
    send_ref[...] = jnp.where(core == 0, sums[1], sums[0])


def thin_kernel(sc, halo_ref, own_ref, after, thin, thin_ref, sem):
    del after
    comps, quarter, _ = thin.shape
    size = 4 * quarter
    rows = comps * size
    part = halo_ref.shape[1]
    core = sc[0]
    tail = halo_ref[rows:].astype(F32)
    per = size // part
    low = jnp.concatenate([tail[i : i + 1] for i in range(per)], axis=1)
    high = jnp.concatenate([tail[per + i : per + i + 1] for i in range(per)], axis=1)
    mine = high == jnp.where(core == 0, 2.0, 0.0)
    place = count_before(mine.astype(F32))
    shape = (quarter, size)
    seats = jnp.broadcast_to(jnp.where(mine, place, -1.0), shape)
    into = (seats == iota(shape, 0).astype(F32)).astype(F32).astype(BF16)
    pack = dot(into, chosen(as_column(low), size)).astype(BF16)
    for comp in range(comps):
        thin_ref[comp] = dot(pack, own_ref[comp * size : (comp + 1) * size]).astype(BF16)
    copy = pltpu.make_async_copy(thin_ref, thin, sem.at[0])
    copy.start()
    copy.wait()


def near_kernel(
    clusters, planes, sc, near_col, target, keeps, scale, coupling, tiles,
    own, thin, near_z, pair_far, pair, far_z, pair_near,
    total_ref, high_ref, low_ref,
    col_ref, target_ref, keep_ref, scale_ref, coupling_ref, tile_ref, window, blocks,
    sems, tile_sems, small_sems,
):
    count, rows, _ = tiles.shape
    columns = own.shape[1]
    size = rows // 3
    quarter = size // 4
    core = sc[0]
    pairs = (
        (near_col, col_ref), (target, target_ref), (keeps, keep_ref), (scale, scale_ref),
        (coupling, coupling_ref),
    )
    smalls = [pltpu.make_async_copy(a, b, small_sems.at[i]) for i, (a, b) in enumerate(pairs)]
    for copy in smalls:
        copy.start()
    seats = (thin, near_z, pair_far, own, pair, far_z, pair_near)
    for j in range(count):
        pltpu.make_async_copy(tiles.at[j], tile_ref.at[j], tile_sems.at[j]).start()
    smalls[0].wait()
    offs = []
    for j in range(count):
        off = col_ref[0, j] - sc[3] + 2
        off = jnp.where(off < 0, off + clusters, off)
        off = jnp.where(off >= clusters, off - clusters, off) - 2
        offs.append(jnp.where(core == 0, off, -off))
    for j in range(count):
        for o in range(-2, 3):

            @pl.when(offs[j] == o)
            def _(j=j, o=o):
                for w in range(3):
                    source = seats[o + 2 + w]
                    if o + w == -2:
                        for comp in range(3):
                            pltpu.make_async_copy(
                                source.at[comp],
                                window.at[j, w, pl.ds(comp * size, quarter)],
                                sems.at[j, w, comp],
                            ).start()
                            window[j, w, comp * size + quarter : (comp + 1) * size] = jnp.zeros(
                                (size - quarter, columns), BF16
                            )
                    else:
                        pltpu.make_async_copy(source, window.at[j, w], sems.at[j, w, 0]).start()

    for copy in smalls[1:]:
        copy.wait()
    far_count, rank, _ = coupling_ref.shape
    width = high_ref.shape[1]
    lane = iota((rank, width), 1)
    for b in range(far_count):
        goal = target_ref[0, b]
        start = jnp.where(goal < 2, 0, lax.rem(goal - 2 - sc[2] + planes, planes)) * rank
        tile = coupling_ref[b].astype(F32) * scale_ref[0, b]
        tile = jnp.concatenate([tile] * (width // rank), axis=1)
        tile = jnp.where((lane >= start) & (lane < start + keep_ref[0, b]), tile, 0.0)
        high = tile.astype(BF16)
        high_ref[b * rank : (b + 1) * rank] = high
        low_ref[b * rank : (b + 1) * rank] = (tile - high.astype(F32)).astype(BF16)

    for j in range(count):
        edge = offs[j] == -2
        for w in range(1, 3):
            pltpu.make_async_copy(own, window.at[j, w], sems.at[j, w, 0]).wait()

        @pl.when(edge)
        def _(j=j):
            for comp in range(3):
                pltpu.make_async_copy(
                    thin.at[comp], window.at[j, 0, pl.ds(comp * size, quarter)], sems.at[j, 0, comp]
                ).wait()

        @pl.when(jnp.logical_not(edge))
        def _(j=j):
            pltpu.make_async_copy(own, window.at[j, 0], sems.at[j, 0, 0]).wait()

        tail = window[j, 1, rows:].astype(F32)
        low, high = tail[0:1, :size], tail[1:2, :size]
        seat = jnp.where(core == 0, high, 2.0 - high)
        first = seat == 0.0
        place = count_before(first.astype(F32))
        low = jnp.where(jnp.logical_and(first, edge), place, low)
        pick = chosen(as_column(seat * size + low), 3 * size)
        for comp in range(3):
            span = slice(comp * size, (comp + 1) * size)
            got = dot(pick[:, :size], window[j, 0, span])
            for w in range(1, 3):
                got += dot(pick[:, w * size : (w + 1) * size], window[j, w, span])
            blocks[j, span] = got.astype(BF16)
    for j in range(count):
        pltpu.make_async_copy(tiles.at[j], tile_ref.at[j], tile_sems.at[j]).wait()
    for r in range(3):
        span = slice(r * size, (r + 1) * size)
        total = dot(tile_ref[0, span], blocks[0])
        for j in range(1, count):
            total += dot(tile_ref[j, span], blocks[j])
        total_ref[span] = total


def reduce_kernel(many, sums, many_ref, sums_ref, sem):
    copy = pltpu.make_async_copy(many, many_ref, sem.at[0])
    copy.start()
    copy.wait()
    total = many_ref[0]
    for i in range(1, many_ref.shape[0]):
        total += many_ref[i]
    for i in range(sums_ref.shape[0]):
        sums_ref[i] = total
    copy = pltpu.make_async_copy(sums_ref, sums, sem.at[1])
    copy.start()
    copy.wait()


def mix_kernel(
    planes, sc, near, sums, basis, high_ref, low_ref, split,
    near_ref, sums_ref, basis_ref, table_ref, coupled_ref, result, in_sems, sems,
):
    pairs = ((sums, sums_ref), (basis, basis_ref), (near, near_ref))
    copies = [pltpu.make_async_copy(a, b, in_sems.at[i]) for i, (a, b) in enumerate(pairs)]
    for copy in copies:
        copy.start()
    copies[0].wait()
    groups, rows, part = split.shape
    rank = sums_ref.shape[1]
    plane = sc[2]
    half = planes // 2
    other = jnp.where(plane < half, half, 0)
    for y in range(groups):
        lanes = slice(y * part, (y + 1) * part)
        base = y * 2 * planes
        coarse = sums_ref[base + 2 * other]
        for i in range(1, half):
            coarse += sums_ref[base + 2 * (other + i)]
        table_ref[:rank, lanes] = coarse
        for i in range(1, planes):
            at = lax.rem(plane + i, planes)
            table_ref[i * rank : (i + 1) * rank, lanes] = sums_ref[base + 2 * at + 1]
    table = table_ref[...]
    high = table.astype(BF16)
    low = (table - high.astype(F32)).astype(BF16)
    step = high_ref.shape[0] // 2
    for i in range(2):
        span = slice(i * step, (i + 1) * step)
        coupled = dot(high_ref[span], high) + dot(high_ref[span], low) + dot(low_ref[span], high)
        coupled_ref[span] = coupled.astype(BF16)
    copies[1].wait()
    copies[2].wait()
    outs = []
    size = rows // 3
    for r in range(3):
        span = slice(r * size, (r + 1) * size)
        total = near_ref[span] + lax.dot_general(
            basis_ref[:, span], coupled_ref[...], (((0,), (0,)), ((), ())), preferred_element_type=F32
        )
        for i in range(groups):
            result[i, span] = total[:, i * part : (i + 1) * part].astype(BF16)
        here = pl.ds(r * size, size)
        outs.append(pltpu.make_async_copy(result.at[:, here], split.at[:, here], sems.at[r]))
        outs[-1].start()
    for copy in outs:
        copy.wait()


def last_kernel(arrived_ref, out_ref):
    total = arrived_ref[0].astype(F32)
    for i in range(1, arrived_ref.shape[0]):
        total += arrived_ref[i].astype(F32)
    out_ref[...] = total


def tie_kernel(*refs):
    del refs


def cost_of(flops):
    return pl.CostEstimate(flops=flops, bytes_accessed=10**6, transcendentals=0)


def tied(value, *after, flops=0):
    return pl.pallas_call(
        tie_kernel,
        out_shape=shape_of(value.shape, value.dtype),
        in_specs=[ANY] * (1 + len(after)),
        out_specs=ANY,
        input_output_aliases={0: 0},
        compiler_params=params(1),
        cost_estimate=cost_of(flops),
        name="tie",
    )(value, *after)


def in_hbm(*values):
    return [pltpu.with_memory_space_constraint(v, pltpu.MemorySpace.HBM) for v in values]


def shape_of(dims, dtype):
    return jax.ShapeDtypeStruct(dims, dtype)


def on_device(
    forces, order, bases, near_tiles, near_col, far_basis, far_coupling, far_scale, far_rank, far_target
):
    clusters = lax.axis_size(CLU)
    planes = lax.axis_size("clu_0")
    steps = lax.axis_size("clu_1")
    groups = lax.axis_size("grp")
    size = order.shape[0]
    comps, _, columns = forces.shape
    rows = comps * size
    part = columns // groups
    _, rank = bases.shape[:2]
    count = near_tiles.shape[1]
    far_count = far_target.shape[1]
    width = planes * rank
    sc = jnp.stack(
        [lax.axis_index("clu_2"), lax.axis_index("grp"), lax.axis_index("clu_0"), lax.axis_index(CLU)]
    ).astype(jnp.int32)

    def swapped(v):
        return lax.ppermute(v, "clu_2", [(0, 1), (1, 0)])

    def sent(v, by):
        pairs = [(i, (i + by if i % 2 else i - by) % clusters) for i in range(clusters)]
        return lax.ppermute(v, CLU, pairs)

    def exchanged(v, axis):
        return lax.all_to_all(v, axis, split_axis=0, concat_axis=0, tiled=True)

    chain = forces.reshape(rows, columns)
    halo, block = pl.pallas_call(
        functools.partial(dress_kernel, clusters),
        out_shape=(shape_of((rows + PAD, part), BF16), shape_of((rows + PAD, columns), BF16)),
        in_specs=[SMEM, HBM, HBM],
        out_specs=(VMEM, HBM),
        scratch_shapes=[
            pltpu.VMEM((1, size), jnp.int32),
            pltpu.VMEM((PAD, columns), BF16),
            pltpu.SemaphoreType.DMA((4,)),
        ],
        compiler_params=params(4),
        name="dress",
    )(sc, *in_hbm(order.reshape(1, size), chain))
    halo = sent(halo, 1)
    block = tied(block, flops=12 * 10**9)
    pair = swapped(block)
    near_z = sent(block, -2)
    far_z = sent(block, 2)

    keep, send = pl.pallas_call(
        pieces_kernel,
        out_shape=(shape_of((rank, part), F32),) * 2,
        in_specs=[SMEM, VMEM, VMEM, VMEM, VMEM],
        out_specs=(VMEM, VMEM),
        compiler_params=params(12),
        cost_estimate=cost_of(10 * 10**9),
        name="pieces",
    )(sc, halo, block, pair, bases.transpose(0, 2, 1, 3))
    level_sum = keep + swapped(send)
    many = exchanged(jnp.broadcast_to(level_sum, (steps, rank, part)), "clu_1")
    thin = pl.pallas_call(
        thin_kernel,
        out_shape=shape_of((comps, size // 4, columns), BF16),
        in_specs=[SMEM, VMEM, VMEM, ANY],
        out_specs=HBM,
        scratch_shapes=[
            pltpu.VMEM((comps, size // 4, columns), BF16),
            pltpu.SemaphoreType.DMA((1,)),
        ],
        compiler_params=params(12),
        name="thin",
    )(sc, halo, block, level_sum)
    thin = sent(thin, 3)
    many = tied(*in_hbm(many), near_z, far_z)
    pair_near = swapped(near_z)
    pair_far = swapped(far_z)
    fan = groups * 2 * planes
    sums = pl.pallas_call(
        reduce_kernel,
        out_shape=shape_of((fan, rank, part), F32),
        in_specs=[ANY],
        out_specs=HBM,
        scratch_shapes=[
            pltpu.VMEM((steps, rank, part), F32),
            pltpu.VMEM((fan, rank, part), F32),
            pltpu.SemaphoreType.DMA((2,)),
        ],
        compiler_params=params(58),
        name="reduce",
    )(many)
    sums = exchanged(sums, ("grp", "clu_0", "clu_2"))
    near, high, low = pl.pallas_call(
        functools.partial(near_kernel, clusters, planes),
        out_shape=(shape_of((rows, columns), F32),) + (shape_of((far_count * rank, width), BF16),) * 2,
        in_specs=[SMEM] + [HBM] * 6 + [ANY] * 7,
        out_specs=(VMEM, VMEM, VMEM),
        scratch_shapes=[
            pltpu.SMEM((1, count), jnp.int32),
            pltpu.SMEM((1, far_count), jnp.int32),
            pltpu.SMEM((1, far_count), jnp.int32),
            pltpu.SMEM((1, far_count), F32),
            pltpu.VMEM((far_count, rank, rank), BF16),
            pltpu.VMEM((count, rows, rows), BF16),
            pltpu.VMEM((count, 3, rows + PAD, columns), BF16),
            pltpu.VMEM((count, rows, columns), BF16),
            pltpu.SemaphoreType.DMA((count, 3, 3)),
            pltpu.SemaphoreType.DMA((count,)),
            pltpu.SemaphoreType.DMA((5,)),
        ],
        compiler_params=params(48),
        cost_estimate=cost_of(12 * 10**9),
        name="near",
    )(
        sc, *in_hbm(near_col, far_target, far_rank, far_scale, far_coupling[0], near_tiles[0]),
        block, *in_hbm(thin), near_z, pair_far, pair, far_z, pair_near,
    )
    split = pl.pallas_call(
        functools.partial(mix_kernel, planes),
        out_shape=shape_of((groups, rows, part), BF16),
        in_specs=[SMEM, HBM, HBM, HBM, VMEM, VMEM],
        out_specs=HBM,
        scratch_shapes=[
            pltpu.VMEM((rows, columns), F32),
            pltpu.VMEM((fan, rank, part), F32),
            pltpu.VMEM((far_count * rank, rows), BF16),
            pltpu.VMEM((width, columns), F32),
            pltpu.VMEM((far_count * rank, columns), BF16),
            pltpu.VMEM((groups, rows, part), BF16),
            pltpu.SemaphoreType.DMA((3,)),
            pltpu.SemaphoreType.DMA((3,)),
        ],
        compiler_params=params(16),
        name="mix",
    )(sc, *in_hbm(near, sums, far_basis.reshape(far_count * rank, rows)), high, low)
    arrived = exchanged(split, "grp")
    velocity = pl.pallas_call(
        last_kernel,
        out_shape=shape_of((rows, part), F32),
        in_specs=[VMEM],
        out_specs=VMEM,
        compiler_params=params(4),
        name="last",
    )(arrived)
    return velocity.reshape(comps, size, part)


def solution(mesh):
    clusters = mesh.shape["clu"]
    torus = Mesh(
        mesh.devices.reshape(mesh.shape["grp"], 4, clusters // 8, 2),
        ("grp", "clu_0", "clu_1", "clu_2"),
    )
    in_specs = (
        P(None, CLU, None),
        P(CLU),
        P(None, None, None, CLU),
        P(CLU, "grp", None, None),
        P(CLU, "grp"),
        P(CLU, "grp", None, None),
        P(CLU, "grp", None, None),
        P(CLU, "grp"),
        P(CLU, "grp"),
        P(CLU, "grp"),
    )
    return jax.shard_map(
        on_device, mesh=torus, in_specs=in_specs, out_specs=P(None, CLU, "grp"), check_vma=False
    )
```

```python
import functools

import jax
import jax.numpy as jnp
from jax import lax
from jax.experimental import pallas as pl
from jax.experimental.pallas import tpu as pltpu
from jax.sharding import Mesh
from jax.sharding import PartitionSpec as P

CLU = ("clu_0", "clu_1", "clu_2")
PAD = 16
F32 = jnp.float32
BF16 = jnp.bfloat16
VMEM = pl.BlockSpec(memory_space=pltpu.VMEM)
SMEM = pl.BlockSpec(memory_space=pltpu.SMEM)
ANY = pl.BlockSpec(memory_space=pl.ANY)
HBM = pl.BlockSpec(memory_space=pltpu.MemorySpace.HBM)


def params(mib):
    return pltpu.CompilerParams(vmem_limit_bytes=mib * 2**20)


def iota(shape, dim):
    return lax.broadcasted_iota(jnp.int32, shape, dim)


def dot(a, b):
    return jnp.dot(a, b, preferred_element_type=F32)


def as_column(row):
    size = row.shape[1]
    square = (size, size)
    spread = jnp.where(iota(square, 0) == iota(square, 1), jnp.broadcast_to(row, square), 0.0)
    return jnp.sum(spread, axis=1, keepdims=True)


def count_before(mask):
    size = mask.shape[1]
    square = (size, size)
    upto = (iota(square, 0) <= iota(square, 1)).astype(F32).astype(BF16)
    rows = jnp.broadcast_to(mask, (16, size)).astype(BF16)
    return dot(rows, upto)[:1] - 1.0


def chosen(column, width):
    shape = (column.shape[0], width)
    return (jnp.broadcast_to(column, shape) == iota(shape, 1).astype(F32)).astype(F32).astype(BF16)


def rows_of(v, width):
    return [v[:, i : i + width] for i in range(0, v.shape[1], width)]


def stacked(lines, width):
    at = iota((PAD, width), 0)
    out = jnp.zeros((PAD, width), F32)
    for i, v in enumerate(lines):
        if v.shape[1] < width:
            v = jnp.concatenate([v, jnp.zeros((1, width - v.shape[1]), F32)], axis=1)
        out = jnp.where(at == i, v, out)
    return out.astype(BF16)


def dress_kernel(clusters, sc, order, forces, halo_ref, block, order_ref, lines_ref, sems):
    rows, columns = forces.shape
    size = order.shape[1]
    part = halo_ref.shape[1]
    start = pl.multiple_of(sc[1] * part, part)
    copies = [
        pltpu.make_async_copy(order, order_ref, sems.at[0]),
        pltpu.make_async_copy(forces.at[:, pl.ds(start, part)], halo_ref.at[pl.ds(0, rows)], sems.at[1]),
        pltpu.make_async_copy(forces, block.at[pl.ds(0, rows)], sems.at[2]),
    ]
    for copy in copies:
        copy.start()
    copies[0].wait()
    rel = order_ref[...] - (sc[3] - 1) * size
    rel = jnp.where(rel < 0, rel + clusters * size, rel)
    rel = jnp.where(rel >= clusters * size, rel - clusters * size, rel)
    high = (rel >= size).astype(jnp.int32) + (rel >= 2 * size).astype(jnp.int32)
    low = (rel - high * size).astype(F32)
    high = high.astype(F32)
    lines_ref[...] = stacked([low, high], columns)
    copy = pltpu.make_async_copy(lines_ref, block.at[pl.ds(rows, PAD)], sems.at[3])
    copy.start()
    halo_ref[rows:] = stacked(rows_of(low, part) + rows_of(high, part), part)
    copy.wait()
    copies[1].wait()
    copies[2].wait()


def pieces_kernel(sc, halo_ref, own_ref, pair_ref, bases_ref, keep_ref, send_ref):
    levels, comps, rank, size = bases_ref.shape
    rows = comps * size
    part = halo_ref.shape[1]
    core = sc[0]
    start = pl.multiple_of(sc[1] * part, part)
    tail = own_ref[rows:].astype(F32)
    low, high = tail[0:1, :size], tail[1:2, :size]
    seat = jnp.where(core == 0, high, 2.0 - high)
    pick = chosen(as_column(seat * size + low), 3 * size)
    sums = [jnp.zeros((rank, part), F32) for _ in range(levels)]
    for comp in range(comps):
        span = slice(comp * size, (comp + 1) * size)
        got = dot(pick[:, :size], halo_ref[span])
        got += dot(pick[:, size : 2 * size], own_ref[span, pl.ds(start, part)])
        got += dot(pick[:, 2 * size :], pair_ref[span, pl.ds(start, part)])
        got = got.astype(BF16)
        for level in range(levels):
            sums[level] += dot(bases_ref[level, comp], got)
    keep_ref[...] = jnp.where(core == 0, sums[0], sums[1])
    send_ref[...] = jnp.where(core == 0, sums[1], sums[0])


def thin_kernel(sc, halo_ref, own_ref, after, thin, thin_ref, sem):
    del after
    comps, quarter, _ = thin.shape
    size = 4 * quarter
    rows = comps * size
    part = halo_ref.shape[1]
    core = sc[0]
    tail = halo_ref[rows:].astype(F32)
    per = size // part
    low = jnp.concatenate([tail[i : i + 1] for i in range(per)], axis=1)
    high = jnp.concatenate([tail[per + i : per + i + 1] for i in range(per)], axis=1)
    mine = high == jnp.where(core == 0, 2.0, 0.0)
    place = count_before(mine.astype(F32))
    shape = (quarter, size)
    seats = jnp.broadcast_to(jnp.where(mine, place, -1.0), shape)
    into = (seats == iota(shape, 0).astype(F32)).astype(F32).astype(BF16)
    pack = dot(into, chosen(as_column(low), size)).astype(BF16)
    for comp in range(comps):
        thin_ref[comp] = dot(pack, own_ref[comp * size : (comp + 1) * size]).astype(BF16)
    copy = pltpu.make_async_copy(thin_ref, thin, sem.at[0])
    copy.start()
    copy.wait()


def near_kernel(
    clusters, sc, near_col, tiles, own, thin, near_z, pair_far, pair, far_z, pair_near,
    total, tile_ref, tails, window, blocks, total_ref, sems, tail_sems, tile_sems, out_sems,
):
    count, rows, _ = tiles.shape
    columns = own.shape[1]
    size = rows // 3
    quarter = size // 4
    core = sc[0]
    seats = (thin, near_z, pair_far, own, pair, far_z, pair_near)
    offs = []
    for j in range(count):
        off = near_col[j] - sc[3] + 2
        off = jnp.where(off < 0, off + clusters, off)
        off = jnp.where(off >= clusters, off - clusters, off) - 2
        offs.append(jnp.where(core == 0, off, -off))
    for j in range(count):
        for o in range(-2, 3):

            @pl.when(offs[j] == o)
            def _(j=j, o=o):
                pltpu.make_async_copy(seats[o + 3].at[pl.ds(rows, PAD)], tails.at[j], tail_sems.at[j]).start()
                for comp in range(3):
                    for w in range(3):
                        source = seats[o + 2 + w]
                        if o + w == -2:
                            pltpu.make_async_copy(
                                source.at[comp],
                                window.at[j, comp, pl.ds(w * size, quarter)],
                                sems.at[j, comp, w],
                            ).start()
                            window[j, comp, w * size + quarter : (w + 1) * size] = jnp.zeros(
                                (size - quarter, columns), BF16
                            )
                        else:
                            pltpu.make_async_copy(
                                source.at[pl.ds(comp * size, size)],
                                window.at[j, comp, pl.ds(w * size, size)],
                                sems.at[j, comp, w],
                            ).start()

    for j in range(count):
        pltpu.make_async_copy(
            tiles.at[j], tile_ref.at[:, pl.ds(j * rows, rows)], tile_sems.at[j]
        ).start()
    for j in range(count):
        edge = offs[j] == -2
        pltpu.make_async_copy(own.at[pl.ds(rows, PAD)], tails.at[j], tail_sems.at[j]).wait()
        tail = tails[j].astype(F32)
        low, high = tail[0:1, :size], tail[1:2, :size]
        seat = jnp.where(core == 0, high, 2.0 - high)
        first = seat == 0.0
        place = count_before(first.astype(F32))
        low = jnp.where(jnp.logical_and(first, edge), place, low)
        pick = chosen(as_column(seat * size + low), 3 * size)
        for comp in range(3):

            @pl.when(edge)
            def _(j=j, comp=comp):
                pltpu.make_async_copy(
                    thin.at[comp], window.at[j, comp, pl.ds(0, quarter)], sems.at[j, comp, 0]
                ).wait()

            @pl.when(jnp.logical_not(edge))
            def _(j=j, comp=comp):
                pltpu.make_async_copy(
                    own.at[pl.ds(0, size)], window.at[j, comp, pl.ds(0, size)], sems.at[j, comp, 0]
                ).wait()

            for w in range(1, 3):
                pltpu.make_async_copy(
                    own.at[pl.ds(0, size)], window.at[j, comp, pl.ds(w * size, size)], sems.at[j, comp, w]
                ).wait()
            at = j * rows + comp * size
            blocks[at : at + size] = dot(pick, window[j, comp]).astype(BF16)
    for j in range(count):
        pltpu.make_async_copy(
            tiles.at[j], tile_ref.at[:, pl.ds(j * rows, rows)], tile_sems.at[j]
        ).wait()
    outs = []
    for r in range(3):
        span = slice(r * size, (r + 1) * size)
        total_ref[span] = dot(tile_ref[span], blocks[...])
        here = pl.ds(r * size, size)
        outs.append(pltpu.make_async_copy(total_ref.at[here], total.at[here], out_sems.at[r]))
        outs[-1].start()
    for copy in outs:
        copy.wait()


def couple_kernel(
    planes, sc, target, keeps, scale, coupling, after, mixed, coupling_ref, mixed_ref, sems
):
    del after
    copy = pltpu.make_async_copy(coupling, coupling_ref, sems.at[0])
    copy.start()
    copy.wait()
    blocks, rank, _ = coupling_ref.shape
    width = mixed_ref.shape[1] // 3
    lane = iota((rank, width), 1)
    for b in range(blocks):
        goal = target[b]
        first = jnp.where(goal < 2, 0, lax.rem(goal - 2 - sc[2] + planes, planes)) * rank
        tile = coupling_ref[b].astype(F32) * scale[b]
        tile = jnp.concatenate([tile] * (width // rank), axis=1)
        tile = jnp.where((lane >= first) & (lane < first + keeps[b]), tile, 0.0)
        high = tile.astype(BF16)
        at = slice(b * rank, (b + 1) * rank)
        mixed_ref[at, :width] = high
        mixed_ref[at, width : 2 * width] = high
        mixed_ref[at, 2 * width :] = (tile - high.astype(F32)).astype(BF16)
    copy = pltpu.make_async_copy(mixed_ref, mixed, sems.at[1])
    copy.start()
    copy.wait()


def reduce_kernel(many_ref, sums, sums_ref, sem):
    total = many_ref[0]
    for i in range(1, many_ref.shape[0]):
        total += many_ref[i]
    for i in range(sums_ref.shape[0]):
        sums_ref[i] = total
    copy = pltpu.make_async_copy(sums_ref, sums, sem.at[0])
    copy.start()
    copy.wait()


def mix_kernel(
    planes, sc, near, sums, basis, mixed, split,
    near_ref, sums_ref, basis_ref, mixed_ref, table_ref, stack_ref, coupled_ref, result, in_sems, sems,
):
    pairs = ((sums, sums_ref), (basis, basis_ref), (near, near_ref), (mixed, mixed_ref))
    copies = [pltpu.make_async_copy(a, b, in_sems.at[i]) for i, (a, b) in enumerate(pairs)]
    for copy in copies:
        copy.start()
    copies[0].wait()
    groups, rows, part = split.shape
    rank = sums_ref.shape[1]
    plane = sc[2]
    half = planes // 2
    other = jnp.where(plane < half, half, 0)
    for y in range(groups):
        lanes = slice(y * part, (y + 1) * part)
        base = y * 2 * planes
        coarse = sums_ref[base + 2 * other]
        for i in range(1, half):
            coarse += sums_ref[base + 2 * (other + i)]
        table_ref[:rank, lanes] = coarse
        for i in range(1, planes):
            at = lax.rem(plane + i, planes)
            table_ref[i * rank : (i + 1) * rank, lanes] = sums_ref[base + 2 * at + 1]
    table = table_ref[...]
    width = table.shape[0]
    high = table.astype(BF16)
    stack_ref[:width] = high
    stack_ref[width : 2 * width] = (table - high.astype(F32)).astype(BF16)
    stack_ref[2 * width :] = high
    copies[3].wait()
    step = mixed_ref.shape[0] // 2
    for i in range(2):
        span = slice(i * step, (i + 1) * step)
        coupled_ref[span] = dot(mixed_ref[span], stack_ref[...]).astype(BF16)
    copies[1].wait()
    copies[2].wait()
    outs = []
    size = rows // 3
    for r in range(3):
        span = slice(r * size, (r + 1) * size)
        total = near_ref[span] + lax.dot_general(
            basis_ref[:, span], coupled_ref[...], (((0,), (0,)), ((), ())), preferred_element_type=F32
        )
        for i in range(groups):
            result[i, span] = total[:, i * part : (i + 1) * part].astype(BF16)
        here = pl.ds(r * size, size)
        outs.append(pltpu.make_async_copy(result.at[:, here], split.at[:, here], sems.at[r]))
        outs[-1].start()
    for copy in outs:
        copy.wait()


def last_kernel(arrived_ref, out_ref):
    total = arrived_ref[0].astype(F32)
    for i in range(1, arrived_ref.shape[0]):
        total += arrived_ref[i].astype(F32)
    out_ref[...] = total


def tie_kernel(*refs):
    del refs


def cost_of(flops):
    return pl.CostEstimate(flops=flops, bytes_accessed=10**6, transcendentals=0)


def tied(value, *after, flops=0):
    return pl.pallas_call(
        tie_kernel,
        out_shape=shape_of(value.shape, value.dtype),
        in_specs=[ANY] * (1 + len(after)),
        out_specs=ANY,
        input_output_aliases={0: 0},
        compiler_params=params(1),
        cost_estimate=cost_of(flops),
        name="tie",
    )(value, *after)


def in_hbm(*values):
    return [pltpu.with_memory_space_constraint(v, pltpu.MemorySpace.HBM) for v in values]


def shape_of(dims, dtype):
    return jax.ShapeDtypeStruct(dims, dtype)


def on_device(
    forces, order, bases, near_tiles, near_col, far_basis, far_coupling, far_scale, far_rank, far_target
):
    clusters = lax.axis_size(CLU)
    planes = lax.axis_size("clu_0")
    steps = lax.axis_size("clu_1")
    groups = lax.axis_size("grp")
    size = order.shape[0]
    comps, _, columns = forces.shape
    rows = comps * size
    part = columns // groups
    _, rank = bases.shape[:2]
    count = near_tiles.shape[1]
    far_count = far_target.shape[1]
    width = planes * rank
    sc = jnp.stack(
        [lax.axis_index("clu_2"), lax.axis_index("grp"), lax.axis_index("clu_0"), lax.axis_index(CLU)]
    ).astype(jnp.int32)

    def swapped(v):
        return lax.ppermute(v, "clu_2", [(0, 1), (1, 0)])

    def sent(v, by):
        pairs = [(i, (i + by if i % 2 else i - by) % clusters) for i in range(clusters)]
        return lax.ppermute(v, CLU, pairs)

    def exchanged(v, axis):
        return lax.all_to_all(v, axis, split_axis=0, concat_axis=0, tiled=True)

    chain = forces.reshape(rows, columns)
    halo, block = pl.pallas_call(
        functools.partial(dress_kernel, clusters),
        out_shape=(shape_of((rows + PAD, part), BF16), shape_of((rows + PAD, columns), BF16)),
        in_specs=[SMEM, HBM, HBM],
        out_specs=(VMEM, HBM),
        scratch_shapes=[
            pltpu.VMEM((1, size), jnp.int32),
            pltpu.VMEM((PAD, columns), BF16),
            pltpu.SemaphoreType.DMA((4,)),
        ],
        compiler_params=params(4),
        name="dress",
    )(sc, *in_hbm(order.reshape(1, size), chain))
    halo = sent(halo, 1)
    block = tied(block, flops=12 * 10**9)
    pair = swapped(block)
    near_z = sent(block, -2)
    far_z = sent(block, 2)

    keep, send = pl.pallas_call(
        pieces_kernel,
        out_shape=(shape_of((rank, part), F32),) * 2,
        in_specs=[SMEM, VMEM, VMEM, VMEM, VMEM],
        out_specs=(VMEM, VMEM),
        compiler_params=params(12),
        cost_estimate=cost_of(10 * 10**9),
        name="pieces",
    )(sc, halo, block, pair, bases.transpose(0, 2, 1, 3))
    level_sum = keep + swapped(send)
    many = exchanged(jnp.broadcast_to(level_sum, (steps, rank, part)), "clu_1")
    thin = pl.pallas_call(
        thin_kernel,
        out_shape=shape_of((comps, size // 4, columns), BF16),
        in_specs=[SMEM, VMEM, VMEM, ANY],
        out_specs=HBM,
        scratch_shapes=[
            pltpu.VMEM((comps, size // 4, columns), BF16),
            pltpu.SemaphoreType.DMA((1,)),
        ],
        compiler_params=params(12),
        name="thin",
    )(sc, halo, block, level_sum)
    thin = sent(thin, 3)
    many = tied(many, near_z, far_z)
    pair_near = swapped(near_z)
    pair_far = swapped(far_z)
    fan = groups * 2 * planes
    sums = pl.pallas_call(
        reduce_kernel,
        out_shape=shape_of((fan, rank, part), F32),
        in_specs=[VMEM],
        out_specs=HBM,
        scratch_shapes=[pltpu.VMEM((fan, rank, part), F32), pltpu.SemaphoreType.DMA((1,))],
        compiler_params=params(4),
        name="reduce",
    )(many)
    sums = exchanged(sums, ("grp", "clu_0", "clu_2"))
    near = pl.pallas_call(
        functools.partial(near_kernel, clusters),
        out_shape=shape_of((rows, columns), F32),
        in_specs=[SMEM, SMEM, HBM] + [ANY] * 7,
        out_specs=HBM,
        scratch_shapes=[
            pltpu.VMEM((rows, count * rows), BF16),
            pltpu.VMEM((count, PAD, columns), BF16),
            pltpu.VMEM((count, comps, rows, columns), BF16),
            pltpu.VMEM((count * rows, columns), BF16),
            pltpu.VMEM((rows, columns), F32),
            pltpu.SemaphoreType.DMA((count, 3, 3)),
            pltpu.SemaphoreType.DMA((count,)),
            pltpu.SemaphoreType.DMA((count,)),
            pltpu.SemaphoreType.DMA((3,)),
        ],
        compiler_params=params(48),
        cost_estimate=cost_of(12 * 10**9),
        name="near",
    )(
        sc, *in_hbm(near_col[0], near_tiles[0]),
        *in_hbm(block), *in_hbm(thin), *in_hbm(near_z), pair_far, *in_hbm(pair), far_z, pair_near,
    )
    mixed = pl.pallas_call(
        functools.partial(couple_kernel, planes),
        out_shape=shape_of((far_count * rank, 3 * width), BF16),
        in_specs=[SMEM, SMEM, SMEM, SMEM, HBM, ANY],
        out_specs=HBM,
        scratch_shapes=[
            pltpu.VMEM((far_count, rank, rank), BF16),
            pltpu.VMEM((far_count * rank, 3 * width), BF16),
            pltpu.SemaphoreType.DMA((2,)),
        ],
        compiler_params=params(4),
        name="couple",
    )(sc, *in_hbm(far_target[0], far_rank[0], far_scale[0], far_coupling[0]), level_sum)
    split = pl.pallas_call(
        functools.partial(mix_kernel, planes),
        out_shape=shape_of((groups, rows, part), BF16),
        in_specs=[SMEM, ANY, ANY, HBM, ANY],
        out_specs=HBM,
        scratch_shapes=[
            pltpu.VMEM((rows, columns), F32),
            pltpu.VMEM((fan, rank, part), F32),
            pltpu.VMEM((far_count * rank, rows), BF16),
            pltpu.VMEM((far_count * rank, 3 * width), BF16),
            pltpu.VMEM((width, columns), F32),
            pltpu.VMEM((3 * width, columns), BF16),
            pltpu.VMEM((far_count * rank, columns), BF16),
            pltpu.VMEM((groups, rows, part), BF16),
            pltpu.SemaphoreType.DMA((4,)),
            pltpu.SemaphoreType.DMA((3,)),
        ],
        compiler_params=params(16),
        name="mix",
    )(sc, near, sums, *in_hbm(far_basis.reshape(far_count * rank, rows)), mixed)
    arrived = exchanged(split, "grp")
    velocity = pl.pallas_call(
        last_kernel,
        out_shape=shape_of((rows, part), F32),
        in_specs=[VMEM],
        out_specs=VMEM,
        compiler_params=params(4),
        name="last",
    )(arrived)
    return velocity.reshape(comps, size, part)


def solution(mesh):
    clusters = mesh.shape["clu"]
    torus = Mesh(
        mesh.devices.reshape(mesh.shape["grp"], 4, clusters // 8, 2),
        ("grp", "clu_0", "clu_1", "clu_2"),
    )
    in_specs = (
        P(None, CLU, None),
        P(CLU),
        P(None, None, None, CLU),
        P(CLU, "grp", None, None),
        P(CLU, "grp"),
        P(CLU, "grp", None, None),
        P(CLU, "grp", None, None),
        P(CLU, "grp"),
        P(CLU, "grp"),
        P(CLU, "grp"),
    )
    return jax.shard_map(
        on_device, mesh=torus, in_specs=in_specs, out_specs=P(None, CLU, "grp"), check_vma=False
    )
```

```python
import functools

import jax
import jax.numpy as jnp
from jax import lax
from jax.experimental import pallas as pl
from jax.experimental.pallas import tpu as pltpu
from jax.sharding import Mesh
from jax.sharding import PartitionSpec as P

CLU = ("clu_0", "clu_1", "clu_2")
PAD = 16
F32 = jnp.float32
BF16 = jnp.bfloat16
VMEM = pl.BlockSpec(memory_space=pltpu.VMEM)
SMEM = pl.BlockSpec(memory_space=pltpu.SMEM)
ANY = pl.BlockSpec(memory_space=pl.ANY)
HBM = pl.BlockSpec(memory_space=pltpu.MemorySpace.HBM)


def params(mib):
    return pltpu.CompilerParams(vmem_limit_bytes=mib * 2**20)


def iota(shape, dim):
    return lax.broadcasted_iota(jnp.int32, shape, dim)


def dot(a, b):
    return jnp.dot(a, b, preferred_element_type=F32)


def as_column(row):
    size = row.shape[1]
    square = (size, size)
    spread = jnp.where(iota(square, 0) == iota(square, 1), jnp.broadcast_to(row, square), 0.0)
    return jnp.sum(spread, axis=1, keepdims=True)


def count_before(mask):
    size = mask.shape[1]
    square = (size, size)
    upto = (iota(square, 0) <= iota(square, 1)).astype(F32).astype(BF16)
    rows = jnp.broadcast_to(mask, (16, size)).astype(BF16)
    return dot(rows, upto)[:1] - 1.0


def chosen(column, width):
    shape = (column.shape[0], width)
    return (jnp.broadcast_to(column, shape) == iota(shape, 1).astype(F32)).astype(F32).astype(BF16)


def rows_of(v, width):
    return [v[:, i : i + width] for i in range(0, v.shape[1], width)]


def stacked(lines, width):
    at = iota((PAD, width), 0)
    out = jnp.zeros((PAD, width), F32)
    for i, v in enumerate(lines):
        if v.shape[1] < width:
            v = jnp.concatenate([v, jnp.zeros((1, width - v.shape[1]), F32)], axis=1)
        out = jnp.where(at == i, v, out)
    return out.astype(BF16)


def dress_kernel(clusters, sc, order, forces, halo_ref, block, order_ref, lines_ref, sems):
    rows, columns = forces.shape
    size = order.shape[1]
    part = halo_ref.shape[1]
    start = pl.multiple_of(sc[1] * part, part)
    copies = [
        pltpu.make_async_copy(order, order_ref, sems.at[0]),
        pltpu.make_async_copy(forces.at[:, pl.ds(start, part)], halo_ref.at[pl.ds(0, rows)], sems.at[1]),
        pltpu.make_async_copy(forces, block.at[pl.ds(0, rows)], sems.at[2]),
    ]
    for copy in copies:
        copy.start()
    copies[0].wait()
    rel = order_ref[...] - (sc[3] - 1) * size
    rel = jnp.where(rel < 0, rel + clusters * size, rel)
    rel = jnp.where(rel >= clusters * size, rel - clusters * size, rel)
    high = (rel >= size).astype(jnp.int32) + (rel >= 2 * size).astype(jnp.int32)
    low = (rel - high * size).astype(F32)
    high = high.astype(F32)
    lines_ref[...] = stacked([low, high], columns)
    copy = pltpu.make_async_copy(lines_ref, block.at[pl.ds(rows, PAD)], sems.at[3])
    copy.start()
    halo_ref[rows:] = stacked(rows_of(low, part) + rows_of(high, part), part)
    copy.wait()
    copies[1].wait()
    copies[2].wait()


def pieces_kernel(sc, halo_ref, own_ref, pair_ref, bases_ref, keep_ref, send_ref):
    levels, comps, rank, size = bases_ref.shape
    rows = comps * size
    part = halo_ref.shape[1]
    core = sc[0]
    start = pl.multiple_of(sc[1] * part, part)
    tail = own_ref[rows:].astype(F32)
    low, high = tail[0:1, :size], tail[1:2, :size]
    seat = jnp.where(core == 0, high, 2.0 - high)
    pick = chosen(as_column(seat * size + low), 3 * size)
    sums = [jnp.zeros((rank, part), F32) for _ in range(levels)]
    for comp in range(comps):
        span = slice(comp * size, (comp + 1) * size)
        got = dot(pick[:, :size], halo_ref[span])
        got += dot(pick[:, size : 2 * size], own_ref[span, pl.ds(start, part)])
        got += dot(pick[:, 2 * size :], pair_ref[span, pl.ds(start, part)])
        got = got.astype(BF16)
        for level in range(levels):
            sums[level] += dot(bases_ref[level, comp], got)
    keep_ref[...] = jnp.where(core == 0, sums[0], sums[1])
    send_ref[...] = jnp.where(core == 0, sums[1], sums[0])


def thin_kernel(sc, halo_ref, own_ref, after, thin, thin_ref, sem):
    del after
    comps, quarter, _ = thin.shape
    size = 4 * quarter
    rows = comps * size
    part = halo_ref.shape[1]
    core = sc[0]
    tail = halo_ref[rows:].astype(F32)
    per = size // part
    low = jnp.concatenate([tail[i : i + 1] for i in range(per)], axis=1)
    high = jnp.concatenate([tail[per + i : per + i + 1] for i in range(per)], axis=1)
    mine = high == jnp.where(core == 0, 2.0, 0.0)
    place = count_before(mine.astype(F32))
    shape = (quarter, size)
    seats = jnp.broadcast_to(jnp.where(mine, place, -1.0), shape)
    into = (seats == iota(shape, 0).astype(F32)).astype(F32).astype(BF16)
    pack = dot(into, chosen(as_column(low), size)).astype(BF16)
    for comp in range(comps):
        thin_ref[comp] = dot(pack, own_ref[comp * size : (comp + 1) * size]).astype(BF16)
    copy = pltpu.make_async_copy(thin_ref, thin, sem.at[0])
    copy.start()
    copy.wait()


def offsets_of(clusters, sc, near_col, count):
    offs = []
    for j in range(count):
        off = near_col[j] - sc[3] + 2
        off = jnp.where(off < 0, off + clusters, off)
        off = jnp.where(off >= clusters, off - clusters, off) - 2
        offs.append(jnp.where(sc[0] == 0, off, -off))
    return offs


def near_kernel(
    clusters, sc, near_col, tiles, own, near_z, pair_far, pair, far_z, pair_near,
    total, tile_ref, tails, window, blocks, total_ref, sems, tail_sems, tile_sems, out_sems,
):
    count, rows, _ = tiles.shape
    columns = own.shape[1]
    size = rows // 3
    core = sc[0]
    seats = (None, near_z, pair_far, own, pair, far_z, pair_near)
    offs = offsets_of(clusters, sc, near_col, count)
    for j in range(count):
        for o in range(-2, 3):

            @pl.when(offs[j] == o)
            def _(j=j, o=o):
                pltpu.make_async_copy(seats[o + 3].at[pl.ds(rows, PAD)], tails.at[j], tail_sems.at[j]).start()
                for comp in range(3):
                    for w in range(3):
                        source = seats[o + 2 + w]
                        if source is None:
                            window[j, comp, :size] = jnp.zeros((size, columns), BF16)
                        else:
                            pltpu.make_async_copy(
                                source.at[pl.ds(comp * size, size)],
                                window.at[j, comp, pl.ds(w * size, size)],
                                sems.at[j, comp, w],
                            ).start()

    for j in range(count):
        pltpu.make_async_copy(
            tiles.at[j], tile_ref.at[:, pl.ds(j * rows, rows)], tile_sems.at[j]
        ).start()
    for j in range(count):
        edge = offs[j] == -2
        pltpu.make_async_copy(own.at[pl.ds(rows, PAD)], tails.at[j], tail_sems.at[j]).wait()
        tail = tails[j].astype(F32)
        low, high = tail[0:1, :size], tail[1:2, :size]
        seat = jnp.where(core == 0, high, 2.0 - high)
        pick = chosen(as_column(seat * size + low), 3 * size)
        for comp in range(3):

            @pl.when(jnp.logical_not(edge))
            def _(j=j, comp=comp):
                pltpu.make_async_copy(
                    own.at[pl.ds(0, size)], window.at[j, comp, pl.ds(0, size)], sems.at[j, comp, 0]
                ).wait()

            for w in range(1, 3):
                pltpu.make_async_copy(
                    own.at[pl.ds(0, size)], window.at[j, comp, pl.ds(w * size, size)], sems.at[j, comp, w]
                ).wait()
            at = j * rows + comp * size
            blocks[at : at + size] = dot(pick, window[j, comp]).astype(BF16)
    for j in range(count):
        pltpu.make_async_copy(
            tiles.at[j], tile_ref.at[:, pl.ds(j * rows, rows)], tile_sems.at[j]
        ).wait()
    outs = []
    for r in range(3):
        span = slice(r * size, (r + 1) * size)
        total_ref[span] = dot(tile_ref[span], blocks[...])
        here = pl.ds(r * size, size)
        outs.append(pltpu.make_async_copy(total_ref.at[here], total.at[here], out_sems.at[r]))
        outs[-1].start()
    for copy in outs:
        copy.wait()


def couple_kernel(
    planes, sc, target, keeps, scale, coupling, after, mixed, coupling_ref, mixed_ref, sems
):
    del after
    copy = pltpu.make_async_copy(coupling, coupling_ref, sems.at[0])
    copy.start()
    copy.wait()
    blocks, rank, _ = coupling_ref.shape
    width = mixed_ref.shape[1] // 3
    lane = iota((rank, width), 1)
    for b in range(blocks):
        goal = target[b]
        first = jnp.where(goal < 2, 0, lax.rem(goal - 2 - sc[2] + planes, planes)) * rank
        tile = coupling_ref[b].astype(F32) * scale[b]
        tile = jnp.concatenate([tile] * (width // rank), axis=1)
        tile = jnp.where((lane >= first) & (lane < first + keeps[b]), tile, 0.0)
        high = tile.astype(BF16)
        at = slice(b * rank, (b + 1) * rank)
        mixed_ref[at, :width] = high
        mixed_ref[at, width : 2 * width] = high
        mixed_ref[at, 2 * width :] = (tile - high.astype(F32)).astype(BF16)
    copy = pltpu.make_async_copy(mixed_ref, mixed, sems.at[1])
    copy.start()
    copy.wait()


def reduce_kernel(many_ref, sums, sums_ref, sem):
    total = many_ref[0]
    for i in range(1, many_ref.shape[0]):
        total += many_ref[i]
    for i in range(sums_ref.shape[0]):
        sums_ref[i] = total
    copy = pltpu.make_async_copy(sums_ref, sums, sem.at[0])
    copy.start()
    copy.wait()


def mix_kernel(
    clusters, planes, sc, near_col, near, sums, basis, mixed, tiles, thin, near_z, split,
    near_ref, sums_ref, basis_ref, mixed_ref, table_ref, stack_ref, coupled_ref, result,
    tile_ref, thin_ref, tail_ref, edge_ref, in_sems, sems, tile_sems, edge_sems,
):
    count, rows, _ = tiles.shape
    offs = offsets_of(clusters, sc, near_col, count)
    edges = [off == -2 for off in offs]
    some = functools.reduce(jnp.logical_or, edges)

    def edge_copies():
        return (
            pltpu.make_async_copy(thin, thin_ref, edge_sems.at[0]),
            pltpu.make_async_copy(near_z.at[pl.ds(rows, PAD)], tail_ref, edge_sems.at[1]),
        )

    def tile_copy(j):
        return pltpu.make_async_copy(tiles.at[j], tile_ref.at[j], tile_sems.at[j])

    pairs = ((sums, sums_ref), (basis, basis_ref), (near, near_ref), (mixed, mixed_ref))
    copies = [pltpu.make_async_copy(a, b, in_sems.at[i]) for i, (a, b) in enumerate(pairs)]
    for copy in copies:
        copy.start()

    @pl.when(some)
    def _():
        for copy in edge_copies():
            copy.start()

    for j in range(count):

        @pl.when(edges[j])
        def _(j=j):
            tile_copy(j).start()

    copies[0].wait()
    groups, rows, part = split.shape
    rank = sums_ref.shape[1]
    plane = sc[2]
    half = planes // 2
    other = jnp.where(plane < half, half, 0)
    for y in range(groups):
        lanes = slice(y * part, (y + 1) * part)
        base = y * 2 * planes
        coarse = sums_ref[base + 2 * other]
        for i in range(1, half):
            coarse += sums_ref[base + 2 * (other + i)]
        table_ref[:rank, lanes] = coarse
        for i in range(1, planes):
            at = lax.rem(plane + i, planes)
            table_ref[i * rank : (i + 1) * rank, lanes] = sums_ref[base + 2 * at + 1]
    table = table_ref[...]
    width = table.shape[0]
    high = table.astype(BF16)
    stack_ref[:width] = high
    stack_ref[width : 2 * width] = (table - high.astype(F32)).astype(BF16)
    stack_ref[2 * width :] = high
    copies[3].wait()
    step = mixed_ref.shape[0] // 2
    for i in range(2):
        span = slice(i * step, (i + 1) * step)
        coupled_ref[span] = dot(mixed_ref[span], stack_ref[...]).astype(BF16)
    copies[1].wait()
    copies[2].wait()
    size = rows // 3

    @pl.when(some)
    def _():
        for copy in edge_copies():
            copy.wait()
        tail = tail_ref[...].astype(F32)
        first = tail[1:2, :size] == jnp.where(sc[0] == 0, 0.0, 2.0)
        place = jnp.where(first, count_before(first.astype(F32)), -1.0)
        pick = chosen(as_column(place), size // 4)
        for comp in range(3):
            edge_ref[comp * size : (comp + 1) * size] = dot(pick, thin_ref[comp]).astype(BF16)

    for j in range(count):

        @pl.when(edges[j])
        def _(j=j):
            tile_copy(j).wait()
            for r in range(3):
                span = slice(r * size, (r + 1) * size)
                near_ref[span] += dot(tile_ref[j, span], edge_ref[...])

    outs = []
    for r in range(3):
        span = slice(r * size, (r + 1) * size)
        total = near_ref[span] + lax.dot_general(
            basis_ref[:, span], coupled_ref[...], (((0,), (0,)), ((), ())), preferred_element_type=F32
        )
        for i in range(groups):
            result[i, span] = total[:, i * part : (i + 1) * part].astype(BF16)
        here = pl.ds(r * size, size)
        outs.append(pltpu.make_async_copy(result.at[:, here], split.at[:, here], sems.at[r]))
        outs[-1].start()
    for copy in outs:
        copy.wait()


def last_kernel(arrived_ref, out_ref):
    total = arrived_ref[0].astype(F32)
    for i in range(1, arrived_ref.shape[0]):
        total += arrived_ref[i].astype(F32)
    out_ref[...] = total


def tie_kernel(*refs):
    del refs


def cost_of(flops):
    return pl.CostEstimate(flops=flops, bytes_accessed=10**6, transcendentals=0)


def tied(value, *after, flops=0):
    return pl.pallas_call(
        tie_kernel,
        out_shape=shape_of(value.shape, value.dtype),
        in_specs=[ANY] * (1 + len(after)),
        out_specs=ANY,
        input_output_aliases={0: 0},
        compiler_params=params(1),
        cost_estimate=cost_of(flops),
        name="tie",
    )(value, *after)


def in_hbm(*values):
    return [pltpu.with_memory_space_constraint(v, pltpu.MemorySpace.HBM) for v in values]


def shape_of(dims, dtype):
    return jax.ShapeDtypeStruct(dims, dtype)


def on_device(
    forces, order, bases, near_tiles, near_col, far_basis, far_coupling, far_scale, far_rank, far_target
):
    clusters = lax.axis_size(CLU)
    planes = lax.axis_size("clu_0")
    steps = lax.axis_size("clu_1")
    groups = lax.axis_size("grp")
    size = order.shape[0]
    comps, _, columns = forces.shape
    rows = comps * size
    part = columns // groups
    _, rank = bases.shape[:2]
    count = near_tiles.shape[1]
    far_count = far_target.shape[1]
    width = planes * rank
    sc = jnp.stack(
        [lax.axis_index("clu_2"), lax.axis_index("grp"), lax.axis_index("clu_0"), lax.axis_index(CLU)]
    ).astype(jnp.int32)

    def swapped(v):
        return lax.ppermute(v, "clu_2", [(0, 1), (1, 0)])

    def sent(v, by):
        pairs = [(i, (i + by if i % 2 else i - by) % clusters) for i in range(clusters)]
        return lax.ppermute(v, CLU, pairs)

    def exchanged(v, axis):
        return lax.all_to_all(v, axis, split_axis=0, concat_axis=0, tiled=True)

    chain = forces.reshape(rows, columns)
    halo, block = pl.pallas_call(
        functools.partial(dress_kernel, clusters),
        out_shape=(shape_of((rows + PAD, part), BF16), shape_of((rows + PAD, columns), BF16)),
        in_specs=[SMEM, HBM, HBM],
        out_specs=(VMEM, HBM),
        scratch_shapes=[
            pltpu.VMEM((1, size), jnp.int32),
            pltpu.VMEM((PAD, columns), BF16),
            pltpu.SemaphoreType.DMA((4,)),
        ],
        compiler_params=params(4),
        name="dress",
    )(sc, *in_hbm(order.reshape(1, size), chain))
    halo = sent(halo, 1)
    block = tied(block, flops=12 * 10**9)
    pair = swapped(block)
    near_z = sent(block, -2)
    far_z = sent(block, 2)

    keep, send = pl.pallas_call(
        pieces_kernel,
        out_shape=(shape_of((rank, part), F32),) * 2,
        in_specs=[SMEM, VMEM, VMEM, VMEM, VMEM],
        out_specs=(VMEM, VMEM),
        compiler_params=params(12),
        cost_estimate=cost_of(10 * 10**9),
        name="pieces",
    )(sc, halo, block, pair, bases.transpose(0, 2, 1, 3))
    level_sum = keep + swapped(send)
    many = exchanged(jnp.broadcast_to(level_sum, (steps, rank, part)), "clu_1")
    thin = pl.pallas_call(
        thin_kernel,
        out_shape=shape_of((comps, size // 4, columns), BF16),
        in_specs=[SMEM, VMEM, VMEM, ANY],
        out_specs=HBM,
        scratch_shapes=[
            pltpu.VMEM((comps, size // 4, columns), BF16),
            pltpu.SemaphoreType.DMA((1,)),
        ],
        compiler_params=params(12),
        name="thin",
    )(sc, halo, block, level_sum)
    mixed = pl.pallas_call(
        functools.partial(couple_kernel, planes),
        out_shape=shape_of((far_count * rank, 3 * width), BF16),
        in_specs=[SMEM, SMEM, SMEM, SMEM, HBM, ANY],
        out_specs=HBM,
        scratch_shapes=[
            pltpu.VMEM((far_count, rank, rank), BF16),
            pltpu.VMEM((far_count * rank, 3 * width), BF16),
            pltpu.SemaphoreType.DMA((2,)),
        ],
        compiler_params=params(4),
        name="couple",
    )(sc, *in_hbm(far_target[0], far_rank[0], far_scale[0], far_coupling[0]), level_sum)
    many = tied(many, near_z, far_z, thin, mixed)
    thin = sent(thin, 3)
    pair_near = swapped(near_z)
    pair_far = swapped(far_z)
    fan = groups * 2 * planes
    sums = pl.pallas_call(
        reduce_kernel,
        out_shape=shape_of((fan, rank, part), F32),
        in_specs=[VMEM],
        out_specs=HBM,
        scratch_shapes=[pltpu.VMEM((fan, rank, part), F32), pltpu.SemaphoreType.DMA((1,))],
        compiler_params=params(4),
        name="reduce",
    )(many)
    sums = exchanged(sums, ("grp", "clu_0", "clu_2"))
    near = pl.pallas_call(
        functools.partial(near_kernel, clusters),
        out_shape=shape_of((rows, columns), F32),
        in_specs=[SMEM, SMEM, HBM] + [ANY] * 6,
        out_specs=HBM,
        scratch_shapes=[
            pltpu.VMEM((rows, count * rows), BF16),
            pltpu.VMEM((count, PAD, columns), BF16),
            pltpu.VMEM((count, comps, rows, columns), BF16),
            pltpu.VMEM((count * rows, columns), BF16),
            pltpu.VMEM((rows, columns), F32),
            pltpu.SemaphoreType.DMA((count, 3, 3)),
            pltpu.SemaphoreType.DMA((count,)),
            pltpu.SemaphoreType.DMA((count,)),
            pltpu.SemaphoreType.DMA((3,)),
        ],
        compiler_params=params(48),
        cost_estimate=cost_of(4 * 10**9),
        name="near",
    )(
        sc, *in_hbm(near_col[0], near_tiles[0]),
        *in_hbm(block, near_z), pair_far, *in_hbm(pair, far_z), pair_near,
    )
    split = pl.pallas_call(
        functools.partial(mix_kernel, clusters, planes),
        out_shape=shape_of((groups, rows, part), BF16),
        in_specs=[SMEM, SMEM, ANY, ANY, HBM, ANY, HBM, HBM, HBM],
        out_specs=HBM,
        scratch_shapes=[
            pltpu.VMEM((rows, columns), F32),
            pltpu.VMEM((fan, rank, part), F32),
            pltpu.VMEM((far_count * rank, rows), BF16),
            pltpu.VMEM((far_count * rank, 3 * width), BF16),
            pltpu.VMEM((width, columns), F32),
            pltpu.VMEM((3 * width, columns), BF16),
            pltpu.VMEM((far_count * rank, columns), BF16),
            pltpu.VMEM((groups, rows, part), BF16),
            pltpu.VMEM((count, rows, rows), BF16),
            pltpu.VMEM((comps, size // 4, columns), BF16),
            pltpu.VMEM((PAD, columns), BF16),
            pltpu.VMEM((rows, columns), BF16),
            pltpu.SemaphoreType.DMA((4,)),
            pltpu.SemaphoreType.DMA((3,)),
            pltpu.SemaphoreType.DMA((count,)),
            pltpu.SemaphoreType.DMA((2,)),
        ],
        compiler_params=params(24),
        name="mix",
    )(
        sc, *in_hbm(near_col[0]), near, sums, *in_hbm(far_basis.reshape(far_count * rank, rows)), mixed,
        *in_hbm(near_tiles[0], thin, near_z),
    )
    arrived = exchanged(split, "grp")
    velocity = pl.pallas_call(
        last_kernel,
        out_shape=shape_of((rows, part), F32),
        in_specs=[VMEM],
        out_specs=VMEM,
        compiler_params=params(4),
        name="last",
    )(arrived)
    return velocity.reshape(comps, size, part)


def solution(mesh):
    clusters = mesh.shape["clu"]
    torus = Mesh(
        mesh.devices.reshape(mesh.shape["grp"], 4, clusters // 8, 2),
        ("grp", "clu_0", "clu_1", "clu_2"),
    )
    in_specs = (
        P(None, CLU, None),
        P(CLU),
        P(None, None, None, CLU),
        P(CLU, "grp", None, None),
        P(CLU, "grp"),
        P(CLU, "grp", None, None),
        P(CLU, "grp", None, None),
        P(CLU, "grp"),
        P(CLU, "grp"),
        P(CLU, "grp"),
    )
    return jax.shard_map(
        on_device, mesh=torus, in_specs=in_specs, out_specs=P(None, CLU, "grp"), check_vma=False
    )
```

```python
import functools

import jax
import jax.numpy as jnp
from jax import lax
from jax.experimental import pallas as pl
from jax.experimental.pallas import tpu as pltpu
from jax.sharding import Mesh
from jax.sharding import PartitionSpec as P

CLU = ("clu_0", "clu_1", "clu_2")
PAD = 16
F32 = jnp.float32
BF16 = jnp.bfloat16
VMEM = pl.BlockSpec(memory_space=pltpu.VMEM)
SMEM = pl.BlockSpec(memory_space=pltpu.SMEM)
ANY = pl.BlockSpec(memory_space=pl.ANY)
HBM = pl.BlockSpec(memory_space=pltpu.MemorySpace.HBM)


def params(mib):
    return pltpu.CompilerParams(vmem_limit_bytes=mib * 2**20)


def iota(shape, dim):
    return lax.broadcasted_iota(jnp.int32, shape, dim)


def dot(a, b):
    return jnp.dot(a, b, preferred_element_type=F32)


def as_column(row):
    size = row.shape[1]
    square = (size, size)
    spread = jnp.where(iota(square, 0) == iota(square, 1), jnp.broadcast_to(row, square), 0.0)
    return jnp.sum(spread, axis=1, keepdims=True)


def count_before(mask):
    size = mask.shape[1]
    square = (size, size)
    upto = (iota(square, 0) <= iota(square, 1)).astype(F32).astype(BF16)
    rows = jnp.broadcast_to(mask, (16, size)).astype(BF16)
    return dot(rows, upto)[:1] - 1.0


def chosen(column, width):
    shape = (column.shape[0], width)
    return (jnp.broadcast_to(column, shape) == iota(shape, 1).astype(F32)).astype(F32).astype(BF16)


def rows_of(v, width):
    return [v[:, i : i + width] for i in range(0, v.shape[1], width)]


def stacked(lines, width):
    at = iota((PAD, width), 0)
    out = jnp.zeros((PAD, width), F32)
    for i, v in enumerate(lines):
        if v.shape[1] < width:
            v = jnp.concatenate([v, jnp.zeros((1, width - v.shape[1]), F32)], axis=1)
        out = jnp.where(at == i, v, out)
    return out.astype(BF16)


def dress_kernel(clusters, sc, order, forces, halo_ref, block, order_ref, lines_ref, sems):
    rows, columns = forces.shape
    size = order.shape[1]
    part = halo_ref.shape[1]
    start = pl.multiple_of(sc[1] * part, part)
    copies = [
        pltpu.make_async_copy(order, order_ref, sems.at[0]),
        pltpu.make_async_copy(forces.at[:, pl.ds(start, part)], halo_ref.at[pl.ds(0, rows)], sems.at[1]),
        pltpu.make_async_copy(forces, block.at[pl.ds(0, rows)], sems.at[2]),
    ]
    for copy in copies:
        copy.start()
    copies[0].wait()
    rel = order_ref[...] - (sc[3] - 1) * size
    rel = jnp.where(rel < 0, rel + clusters * size, rel)
    rel = jnp.where(rel >= clusters * size, rel - clusters * size, rel)
    high = (rel >= size).astype(jnp.int32) + (rel >= 2 * size).astype(jnp.int32)
    low = (rel - high * size).astype(F32)
    high = high.astype(F32)
    lines_ref[...] = stacked([low, high], columns)
    copy = pltpu.make_async_copy(lines_ref, block.at[pl.ds(rows, PAD)], sems.at[3])
    copy.start()
    halo_ref[rows:] = stacked(rows_of(low, part) + rows_of(high, part), part)
    copy.wait()
    copies[1].wait()
    copies[2].wait()


def pieces_kernel(sc, halo_ref, own_ref, pair_ref, bases_ref, keep_ref, send_ref):
    levels, comps, rank, size = bases_ref.shape
    rows = comps * size
    part = halo_ref.shape[1]
    core = sc[0]
    start = pl.multiple_of(sc[1] * part, part)
    tail = own_ref[rows:].astype(F32)
    low, high = tail[0:1, :size], tail[1:2, :size]
    seat = jnp.where(core == 0, high, 2.0 - high)
    pick = chosen(as_column(seat * size + low), 3 * size)
    sums = [jnp.zeros((rank, part), F32) for _ in range(levels)]
    for comp in range(comps):
        span = slice(comp * size, (comp + 1) * size)
        got = dot(pick[:, :size], halo_ref[span])
        got += dot(pick[:, size : 2 * size], own_ref[span, pl.ds(start, part)])
        got += dot(pick[:, 2 * size :], pair_ref[span, pl.ds(start, part)])
        got = got.astype(BF16)
        for level in range(levels):
            sums[level] += dot(bases_ref[level, comp], got)
    keep_ref[...] = jnp.where(core == 0, sums[0], sums[1])
    send_ref[...] = jnp.where(core == 0, sums[1], sums[0])


def side_kernel(
    planes, sc, target, keeps, scale, coupling, own, halo_ref, after, thin, mixed,
    coupling_ref, own_ref, mixed_ref, thin_ref, sems,
):
    del after
    copy = pltpu.make_async_copy(coupling, coupling_ref, sems.at[0])
    copy.start()
    own_copy = pltpu.make_async_copy(own.at[pl.ds(0, own_ref.shape[0])], own_ref, sems.at[3])
    own_copy.start()
    comps, quarter, _ = thin.shape
    size = 4 * quarter
    rows = comps * size
    part = halo_ref.shape[1]
    core = sc[0]
    tail = halo_ref[rows:].astype(F32)
    per = size // part
    low = jnp.concatenate([tail[i : i + 1] for i in range(per)], axis=1)
    high = jnp.concatenate([tail[per + i : per + i + 1] for i in range(per)], axis=1)
    mine = high == jnp.where(core == 0, 2.0, 0.0)
    place = count_before(mine.astype(F32))
    shape = (quarter, size)
    seats = jnp.broadcast_to(jnp.where(mine, place, -1.0), shape)
    into = (seats == iota(shape, 0).astype(F32)).astype(F32).astype(BF16)
    pack = dot(into, chosen(as_column(low), size)).astype(BF16)
    own_copy.wait()
    for comp in range(comps):
        thin_ref[comp] = dot(pack, own_ref[comp * size : (comp + 1) * size]).astype(BF16)
    thin_copy = pltpu.make_async_copy(thin_ref, thin, sems.at[1])
    thin_copy.start()
    copy.wait()
    blocks, rank, _ = coupling_ref.shape
    width = mixed_ref.shape[1] // 3
    lane = iota((rank, width), 1)
    for b in range(blocks):
        goal = target[b]
        first = jnp.where(goal < 2, 0, lax.rem(goal - 2 - sc[2] + planes, planes)) * rank
        tile = coupling_ref[b].astype(F32) * scale[b]
        tile = jnp.concatenate([tile] * (width // rank), axis=1)
        tile = jnp.where((lane >= first) & (lane < first + keeps[b]), tile, 0.0)
        high = tile.astype(BF16)
        at = slice(b * rank, (b + 1) * rank)
        mixed_ref[at, :width] = high
        mixed_ref[at, width : 2 * width] = high
        mixed_ref[at, 2 * width :] = (tile - high.astype(F32)).astype(BF16)
    copy = pltpu.make_async_copy(mixed_ref, mixed, sems.at[2])
    copy.start()
    copy.wait()
    thin_copy.wait()


def offsets_of(clusters, sc, near_col, count):
    offs = []
    for j in range(count):
        off = near_col[j] - sc[3] + 2
        off = jnp.where(off < 0, off + clusters, off)
        off = jnp.where(off >= clusters, off - clusters, off) - 2
        offs.append(jnp.where(sc[0] == 0, off, -off))
    return offs


def near_kernel(
    clusters, sc, near_col, tiles, own, near_z, pair_far, pair, far_z, pair_near,
    total, tile_ref, tails, window, blocks, total_ref, sems, tail_sems, tile_sems, out_sems,
):
    count, rows, _ = tiles.shape
    columns = own.shape[1]
    size = rows // 3
    core = sc[0]
    seats = (None, near_z, pair_far, own, pair, far_z, pair_near)
    offs = offsets_of(clusters, sc, near_col, count)
    for j in range(count):
        for o in range(-2, 3):

            @pl.when(offs[j] == o)
            def _(j=j, o=o):
                pltpu.make_async_copy(seats[o + 3].at[pl.ds(rows, PAD)], tails.at[j], tail_sems.at[j]).start()
                for comp in range(3):
                    for w in range(3):
                        source = seats[o + 2 + w]
                        if source is None:
                            window[j, comp, :size] = jnp.zeros((size, columns), BF16)
                        else:
                            pltpu.make_async_copy(
                                source.at[pl.ds(comp * size, size)],
                                window.at[j, comp, pl.ds(w * size, size)],
                                sems.at[j, comp, w],
                            ).start()

    for j in range(count):
        pltpu.make_async_copy(
            tiles.at[j], tile_ref.at[:, pl.ds(j * rows, rows)], tile_sems.at[j]
        ).start()
    for j in range(count):
        edge = offs[j] == -2
        pltpu.make_async_copy(own.at[pl.ds(rows, PAD)], tails.at[j], tail_sems.at[j]).wait()
        tail = tails[j].astype(F32)
        low, high = tail[0:1, :size], tail[1:2, :size]
        seat = jnp.where(core == 0, high, 2.0 - high)
        pick = chosen(as_column(seat * size + low), 3 * size)
        for comp in range(3):

            @pl.when(jnp.logical_not(edge))
            def _(j=j, comp=comp):
                pltpu.make_async_copy(
                    own.at[pl.ds(0, size)], window.at[j, comp, pl.ds(0, size)], sems.at[j, comp, 0]
                ).wait()

            for w in range(1, 3):
                pltpu.make_async_copy(
                    own.at[pl.ds(0, size)], window.at[j, comp, pl.ds(w * size, size)], sems.at[j, comp, w]
                ).wait()
            at = j * rows + comp * size
            blocks[at : at + size] = dot(pick, window[j, comp]).astype(BF16)
    for j in range(count):
        pltpu.make_async_copy(
            tiles.at[j], tile_ref.at[:, pl.ds(j * rows, rows)], tile_sems.at[j]
        ).wait()
    outs = []
    for r in range(3):
        span = slice(r * size, (r + 1) * size)
        total_ref[span] = dot(tile_ref[span], blocks[...])
        here = pl.ds(r * size, size)
        outs.append(pltpu.make_async_copy(total_ref.at[here], total.at[here], out_sems.at[r]))
        outs[-1].start()
    for copy in outs:
        copy.wait()


def reduce_kernel(many_ref, sums, sums_ref, sem):
    total = many_ref[0]
    for i in range(1, many_ref.shape[0]):
        total += many_ref[i]
    for i in range(sums_ref.shape[0]):
        sums_ref[i] = total
    copy = pltpu.make_async_copy(sums_ref, sums, sem.at[0])
    copy.start()
    copy.wait()


def mix_kernel(
    clusters, planes, sc, near_col, near, sums, basis, mixed, tiles, thin, near_z, split,
    near_ref, sums_ref, basis_ref, mixed_ref, table_ref, stack_ref, coupled_ref, result,
    tile_ref, thin_ref, tail_ref, edge_ref, in_sems, sems, tile_sems, edge_sems,
):
    count, rows, _ = tiles.shape
    offs = offsets_of(clusters, sc, near_col, count)
    edges = [off == -2 for off in offs]
    some = functools.reduce(jnp.logical_or, edges)

    def edge_copies():
        return (
            pltpu.make_async_copy(thin, thin_ref, edge_sems.at[0]),
            pltpu.make_async_copy(near_z.at[pl.ds(rows, PAD)], tail_ref, edge_sems.at[1]),
        )

    def tile_copy(j):
        return pltpu.make_async_copy(tiles.at[j], tile_ref.at[j], tile_sems.at[j])

    pairs = ((sums, sums_ref), (basis, basis_ref), (near, near_ref), (mixed, mixed_ref))
    copies = [pltpu.make_async_copy(a, b, in_sems.at[i]) for i, (a, b) in enumerate(pairs)]
    for copy in copies:
        copy.start()

    @pl.when(some)
    def _():
        for copy in edge_copies():
            copy.start()

    for j in range(count):

        @pl.when(edges[j])
        def _(j=j):
            tile_copy(j).start()

    copies[0].wait()
    groups, rows, part = split.shape
    rank = sums_ref.shape[1]
    plane = sc[2]
    half = planes // 2
    other = jnp.where(plane < half, half, 0)
    for y in range(groups):
        lanes = slice(y * part, (y + 1) * part)
        base = y * 2 * planes
        coarse = sums_ref[base + 2 * other]
        for i in range(1, half):
            coarse += sums_ref[base + 2 * (other + i)]
        table_ref[:rank, lanes] = coarse
        for i in range(1, planes):
            at = lax.rem(plane + i, planes)
            table_ref[i * rank : (i + 1) * rank, lanes] = sums_ref[base + 2 * at + 1]
    table = table_ref[...]
    width = table.shape[0]
    high = table.astype(BF16)
    stack_ref[:width] = high
    stack_ref[width : 2 * width] = (table - high.astype(F32)).astype(BF16)
    stack_ref[2 * width :] = high
    copies[3].wait()
    step = mixed_ref.shape[0] // 2
    for i in range(2):
        span = slice(i * step, (i + 1) * step)
        coupled_ref[span] = dot(mixed_ref[span], stack_ref[...]).astype(BF16)
    copies[1].wait()
    copies[2].wait()
    size = rows // 3

    @pl.when(some)
    def _():
        for copy in edge_copies():
            copy.wait()
        tail = tail_ref[...].astype(F32)
        first = tail[1:2, :size] == jnp.where(sc[0] == 0, 0.0, 2.0)
        place = jnp.where(first, count_before(first.astype(F32)), -1.0)
        pick = chosen(as_column(place), size // 4)
        for comp in range(3):
            edge_ref[comp * size : (comp + 1) * size] = dot(pick, thin_ref[comp]).astype(BF16)

    for j in range(count):

        @pl.when(edges[j])
        def _(j=j):
            tile_copy(j).wait()
            for r in range(3):
                span = slice(r * size, (r + 1) * size)
                near_ref[span] += dot(tile_ref[j, span], edge_ref[...])

    outs = []
    for r in range(3):
        span = slice(r * size, (r + 1) * size)
        total = near_ref[span] + lax.dot_general(
            basis_ref[:, span], coupled_ref[...], (((0,), (0,)), ((), ())), preferred_element_type=F32
        )
        for i in range(groups):
            result[i, span] = total[:, i * part : (i + 1) * part].astype(BF16)
        here = pl.ds(r * size, size)
        outs.append(pltpu.make_async_copy(result.at[:, here], split.at[:, here], sems.at[r]))
        outs[-1].start()
    for copy in outs:
        copy.wait()


def last_kernel(arrived_ref, out_ref):
    total = arrived_ref[0].astype(F32)
    for i in range(1, arrived_ref.shape[0]):
        total += arrived_ref[i].astype(F32)
    out_ref[...] = total


def tie_kernel(*refs):
    del refs


def cost_of(flops):
    return pl.CostEstimate(flops=flops, bytes_accessed=10**6, transcendentals=0)


def tied(value, *after, flops=0):
    return pl.pallas_call(
        tie_kernel,
        out_shape=shape_of(value.shape, value.dtype),
        in_specs=[ANY] * (1 + len(after)),
        out_specs=ANY,
        input_output_aliases={0: 0},
        compiler_params=params(1),
        cost_estimate=cost_of(flops),
        name="tie",
    )(value, *after)


def in_hbm(*values):
    return [pltpu.with_memory_space_constraint(v, pltpu.MemorySpace.HBM) for v in values]


def shape_of(dims, dtype):
    return jax.ShapeDtypeStruct(dims, dtype)


def on_device(
    forces, order, bases, near_tiles, near_col, far_basis, far_coupling, far_scale, far_rank, far_target
):
    clusters = lax.axis_size(CLU)
    planes = lax.axis_size("clu_0")
    steps = lax.axis_size("clu_1")
    groups = lax.axis_size("grp")
    size = order.shape[0]
    comps, _, columns = forces.shape
    rows = comps * size
    part = columns // groups
    _, rank = bases.shape[:2]
    count = near_tiles.shape[1]
    far_count = far_target.shape[1]
    width = planes * rank
    sc = jnp.stack(
        [lax.axis_index("clu_2"), lax.axis_index("grp"), lax.axis_index("clu_0"), lax.axis_index(CLU)]
    ).astype(jnp.int32)

    def swapped(v):
        return lax.ppermute(v, "clu_2", [(0, 1), (1, 0)])

    def sent(v, by):
        pairs = [(i, (i + by if i % 2 else i - by) % clusters) for i in range(clusters)]
        return lax.ppermute(v, CLU, pairs)

    def exchanged(v, axis):
        return lax.all_to_all(v, axis, split_axis=0, concat_axis=0, tiled=True)

    chain = forces.reshape(rows, columns)
    halo, block = pl.pallas_call(
        functools.partial(dress_kernel, clusters),
        out_shape=(shape_of((rows + PAD, part), BF16), shape_of((rows + PAD, columns), BF16)),
        in_specs=[SMEM, HBM, HBM],
        out_specs=(VMEM, HBM),
        scratch_shapes=[
            pltpu.VMEM((1, size), jnp.int32),
            pltpu.VMEM((PAD, columns), BF16),
            pltpu.SemaphoreType.DMA((4,)),
        ],
        compiler_params=params(4),
        name="dress",
    )(sc, *in_hbm(order.reshape(1, size), chain))
    halo = sent(halo, 1)
    block = tied(block, flops=12 * 10**9)
    pair = swapped(block)
    near_z = sent(block, -2)
    far_z = sent(block, 2)

    keep, send = pl.pallas_call(
        pieces_kernel,
        out_shape=(shape_of((rank, part), F32),) * 2,
        in_specs=[SMEM, VMEM, VMEM, VMEM, VMEM],
        out_specs=(VMEM, VMEM),
        compiler_params=params(12),
        cost_estimate=cost_of(5 * 10**9),
        name="pieces",
    )(sc, halo, block, pair, bases.transpose(0, 2, 1, 3))
    level_sum = keep + swapped(send)
    many = exchanged(jnp.broadcast_to(level_sum, (steps, rank, part)), "clu_1")
    thin, mixed = pl.pallas_call(
        functools.partial(side_kernel, planes),
        out_shape=(
            shape_of((comps, size // 4, columns), BF16),
            shape_of((far_count * rank, 3 * width), BF16),
        ),
        in_specs=[SMEM, SMEM, SMEM, SMEM, HBM, HBM, VMEM, ANY],
        out_specs=(HBM, HBM),
        scratch_shapes=[
            pltpu.VMEM((far_count, rank, rank), BF16),
            pltpu.VMEM((rows, columns), BF16),
            pltpu.VMEM((far_count * rank, 3 * width), BF16),
            pltpu.VMEM((comps, size // 4, columns), BF16),
            pltpu.SemaphoreType.DMA((4,)),
        ],
        compiler_params=params(12),
        name="side",
    )(
        sc, *in_hbm(far_target[0], far_rank[0], far_scale[0], far_coupling[0], block), halo, level_sum,
    )
    many = tied(many, near_z, far_z, thin, mixed)
    thin = sent(thin, 3)
    pair_near = swapped(near_z)
    pair_far = swapped(far_z)
    fan = groups * 2 * planes
    sums = pl.pallas_call(
        reduce_kernel,
        out_shape=shape_of((fan, rank, part), F32),
        in_specs=[VMEM],
        out_specs=HBM,
        scratch_shapes=[pltpu.VMEM((fan, rank, part), F32), pltpu.SemaphoreType.DMA((1,))],
        compiler_params=params(4),
        name="reduce",
    )(many)
    sums = exchanged(sums, ("grp", "clu_0", "clu_2"))
    near = pl.pallas_call(
        functools.partial(near_kernel, clusters),
        out_shape=shape_of((rows, columns), F32),
        in_specs=[SMEM, SMEM, HBM] + [ANY] * 6,
        out_specs=HBM,
        scratch_shapes=[
            pltpu.VMEM((rows, count * rows), BF16),
            pltpu.VMEM((count, PAD, columns), BF16),
            pltpu.VMEM((count, comps, rows, columns), BF16),
            pltpu.VMEM((count * rows, columns), BF16),
            pltpu.VMEM((rows, columns), F32),
            pltpu.SemaphoreType.DMA((count, 3, 3)),
            pltpu.SemaphoreType.DMA((count,)),
            pltpu.SemaphoreType.DMA((count,)),
            pltpu.SemaphoreType.DMA((3,)),
        ],
        compiler_params=params(48),
        cost_estimate=cost_of(4 * 10**9),
        name="near",
    )(
        sc, *in_hbm(near_col[0], near_tiles[0]),
        *in_hbm(block, near_z), pair_far, *in_hbm(pair, far_z), pair_near,
    )
    split = pl.pallas_call(
        functools.partial(mix_kernel, clusters, planes),
        out_shape=shape_of((groups, rows, part), BF16),
        in_specs=[SMEM, SMEM, ANY, ANY, HBM, ANY, HBM, HBM, HBM],
        out_specs=HBM,
        scratch_shapes=[
            pltpu.VMEM((rows, columns), F32),
            pltpu.VMEM((fan, rank, part), F32),
            pltpu.VMEM((far_count * rank, rows), BF16),
            pltpu.VMEM((far_count * rank, 3 * width), BF16),
            pltpu.VMEM((width, columns), F32),
            pltpu.VMEM((3 * width, columns), BF16),
            pltpu.VMEM((far_count * rank, columns), BF16),
            pltpu.VMEM((groups, rows, part), BF16),
            pltpu.VMEM((count, rows, rows), BF16),
            pltpu.VMEM((comps, size // 4, columns), BF16),
            pltpu.VMEM((PAD, columns), BF16),
            pltpu.VMEM((rows, columns), BF16),
            pltpu.SemaphoreType.DMA((4,)),
            pltpu.SemaphoreType.DMA((3,)),
            pltpu.SemaphoreType.DMA((count,)),
            pltpu.SemaphoreType.DMA((2,)),
        ],
        compiler_params=params(24),
        name="mix",
    )(
        sc, *in_hbm(near_col[0]), near, sums, *in_hbm(far_basis.reshape(far_count * rank, rows)), mixed,
        *in_hbm(near_tiles[0], thin, near_z),
    )
    arrived = exchanged(split, "grp")
    velocity = pl.pallas_call(
        last_kernel,
        out_shape=shape_of((rows, part), F32),
        in_specs=[VMEM],
        out_specs=VMEM,
        compiler_params=params(4),
        name="last",
    )(arrived)
    return velocity.reshape(comps, size, part)


def solution(mesh):
    clusters = mesh.shape["clu"]
    torus = Mesh(
        mesh.devices.reshape(mesh.shape["grp"], 4, clusters // 8, 2),
        ("grp", "clu_0", "clu_1", "clu_2"),
    )
    in_specs = (
        P(None, CLU, None),
        P(CLU),
        P(None, None, None, CLU),
        P(CLU, "grp", None, None),
        P(CLU, "grp"),
        P(CLU, "grp", None, None),
        P(CLU, "grp", None, None),
        P(CLU, "grp"),
        P(CLU, "grp"),
        P(CLU, "grp"),
    )
    return jax.shard_map(
        on_device, mesh=torus, in_specs=in_specs, out_specs=P(None, CLU, "grp"), check_vma=False
    )
```

```python
import functools

import jax
import jax.numpy as jnp
from jax import lax
from jax.experimental import pallas as pl
from jax.experimental.pallas import tpu as pltpu
from jax.sharding import Mesh
from jax.sharding import PartitionSpec as P

CLU = ("clu_0", "clu_1", "clu_2")
PAD = 16
F32 = jnp.float32
BF16 = jnp.bfloat16
VMEM = pl.BlockSpec(memory_space=pltpu.VMEM)
SMEM = pl.BlockSpec(memory_space=pltpu.SMEM)
ANY = pl.BlockSpec(memory_space=pl.ANY)
HBM = pl.BlockSpec(memory_space=pltpu.MemorySpace.HBM)


def params(mib):
    return pltpu.CompilerParams(vmem_limit_bytes=mib * 2**20)


def iota(shape, dim):
    return lax.broadcasted_iota(jnp.int32, shape, dim)


def dot(a, b):
    return jnp.dot(a, b, preferred_element_type=F32)


def as_column(row):
    size = row.shape[1]
    square = (size, size)
    spread = jnp.where(iota(square, 0) == iota(square, 1), jnp.broadcast_to(row, square), 0.0)
    return jnp.sum(spread, axis=1, keepdims=True)


def count_before(mask):
    size = mask.shape[1]
    square = (size, size)
    upto = (iota(square, 0) <= iota(square, 1)).astype(F32).astype(BF16)
    rows = jnp.broadcast_to(mask, (16, size)).astype(BF16)
    return dot(rows, upto)[:1] - 1.0


def chosen(column, width):
    shape = (column.shape[0], width)
    return (jnp.broadcast_to(column, shape) == iota(shape, 1).astype(F32)).astype(F32).astype(BF16)


def rows_of(v, width):
    return [v[:, i : i + width] for i in range(0, v.shape[1], width)]


def stacked(lines, width):
    at = iota((PAD, width), 0)
    out = jnp.zeros((PAD, width), F32)
    for i, v in enumerate(lines):
        if v.shape[1] < width:
            v = jnp.concatenate([v, jnp.zeros((1, width - v.shape[1]), F32)], axis=1)
        out = jnp.where(at == i, v, out)
    return out.astype(BF16)


def dress_kernel(clusters, sc, order, forces, halo_ref, block, order_ref, lines_ref, sems):
    rows, columns = forces.shape
    size = order.shape[1]
    part = halo_ref.shape[1]
    start = pl.multiple_of(sc[1] * part, part)
    copies = [
        pltpu.make_async_copy(order, order_ref, sems.at[0]),
        pltpu.make_async_copy(forces.at[:, pl.ds(start, part)], halo_ref.at[pl.ds(0, rows)], sems.at[1]),
        pltpu.make_async_copy(forces, block.at[pl.ds(0, rows)], sems.at[2]),
    ]
    for copy in copies:
        copy.start()
    copies[0].wait()
    rel = order_ref[...] - (sc[3] - 1) * size
    rel = jnp.where(rel < 0, rel + clusters * size, rel)
    rel = jnp.where(rel >= clusters * size, rel - clusters * size, rel)
    high = (rel >= size).astype(jnp.int32) + (rel >= 2 * size).astype(jnp.int32)
    low = (rel - high * size).astype(F32)
    high = high.astype(F32)
    lines_ref[...] = stacked([low, high], columns)
    copy = pltpu.make_async_copy(lines_ref, block.at[pl.ds(rows, PAD)], sems.at[3])
    copy.start()
    halo_ref[rows:] = stacked(rows_of(low, part) + rows_of(high, part), part)
    copy.wait()
    copies[1].wait()
    copies[2].wait()


def pieces_kernel(sc, halo_ref, own_ref, pair_ref, bases_ref, keep_ref, send_ref):
    levels, comps, rank, size = bases_ref.shape
    rows = comps * size
    part = halo_ref.shape[1]
    core = sc[0]
    start = pl.multiple_of(sc[1] * part, part)
    tail = own_ref[rows:].astype(F32)
    low, high = tail[0:1, :size], tail[1:2, :size]
    seat = jnp.where(core == 0, high, 2.0 - high)
    pick = chosen(as_column(seat * size + low), 3 * size)
    sums = [jnp.zeros((rank, part), F32) for _ in range(levels)]
    for comp in range(comps):
        span = slice(comp * size, (comp + 1) * size)
        got = dot(pick[:, :size], halo_ref[span])
        got += dot(pick[:, size : 2 * size], own_ref[span, pl.ds(start, part)])
        got += dot(pick[:, 2 * size :], pair_ref[span, pl.ds(start, part)])
        got = got.astype(BF16)
        for level in range(levels):
            sums[level] += dot(bases_ref[level, comp], got)
    keep_ref[...] = jnp.where(core == 0, sums[0], sums[1])
    send_ref[...] = jnp.where(core == 0, sums[1], sums[0])


def side_kernel(
    planes, sc, target, keeps, scale, coupling, own, halo_ref, after, thin, mixed,
    coupling_ref, own_ref, mixed_ref, thin_ref, sems,
):
    del after
    copy = pltpu.make_async_copy(coupling, coupling_ref, sems.at[0])
    copy.start()
    own_copy = pltpu.make_async_copy(own.at[pl.ds(0, own_ref.shape[0])], own_ref, sems.at[3])
    own_copy.start()
    comps, quarter, _ = thin.shape
    size = 4 * quarter
    rows = comps * size
    part = halo_ref.shape[1]
    core = sc[0]
    tail = halo_ref[rows:].astype(F32)
    per = size // part
    low = jnp.concatenate([tail[i : i + 1] for i in range(per)], axis=1)
    high = jnp.concatenate([tail[per + i : per + i + 1] for i in range(per)], axis=1)
    mine = high == jnp.where(core == 0, 2.0, 0.0)
    place = count_before(mine.astype(F32))
    shape = (quarter, size)
    seats = jnp.broadcast_to(jnp.where(mine, place, -1.0), shape)
    into = (seats == iota(shape, 0).astype(F32)).astype(F32).astype(BF16)
    pack = dot(into, chosen(as_column(low), size)).astype(BF16)
    own_copy.wait()
    for comp in range(comps):
        thin_ref[comp] = dot(pack, own_ref[comp * size : (comp + 1) * size]).astype(BF16)
    thin_copy = pltpu.make_async_copy(thin_ref, thin, sems.at[1])
    thin_copy.start()
    copy.wait()
    blocks, rank, _ = coupling_ref.shape
    width = mixed_ref.shape[1] // 3
    lane = iota((rank, width), 1)
    for b in range(blocks):
        goal = target[b]
        first = jnp.where(goal < 2, 0, lax.rem(goal - 2 - sc[2] + planes, planes)) * rank
        tile = coupling_ref[b].astype(F32) * scale[b]
        tile = jnp.concatenate([tile] * (width // rank), axis=1)
        tile = jnp.where((lane >= first) & (lane < first + keeps[b]), tile, 0.0)
        high = tile.astype(BF16)
        at = slice(b * rank, (b + 1) * rank)
        mixed_ref[at, :width] = high
        mixed_ref[at, width : 2 * width] = high
        mixed_ref[at, 2 * width :] = (tile - high.astype(F32)).astype(BF16)
    copy = pltpu.make_async_copy(mixed_ref, mixed, sems.at[2])
    copy.start()
    copy.wait()
    thin_copy.wait()


def offsets_of(clusters, sc, near_col, count):
    offs = []
    for j in range(count):
        off = near_col[j] - sc[3] + 2
        off = jnp.where(off < 0, off + clusters, off)
        off = jnp.where(off >= clusters, off - clusters, off) - 2
        offs.append(jnp.where(sc[0] == 0, off, -off))
    return offs


def near_kernel(
    clusters, sc, near_col, tiles, own, near_z, pair_far, pair, far_z, pair_near,
    total, tile_ref, tails, window, blocks, total_ref, sems, tail_sems, tile_sems, out_sems,
):
    count, rows, _ = tiles.shape
    columns = own.shape[1]
    size = rows // 3
    core = sc[0]
    seats = (None, near_z, pair_far, own, pair, far_z, pair_near)
    offs = offsets_of(clusters, sc, near_col, count)
    for j in range(count):
        for o in range(-2, 3):

            @pl.when(offs[j] == o)
            def _(j=j, o=o):
                pltpu.make_async_copy(seats[o + 3].at[pl.ds(rows, PAD)], tails.at[j], tail_sems.at[j]).start()
                for comp in range(3):
                    for w in range(3):
                        source = seats[o + 2 + w]
                        if source is None:
                            window[j, comp, :size] = jnp.zeros((size, columns), BF16)
                        else:
                            pltpu.make_async_copy(
                                source.at[pl.ds(comp * size, size)],
                                window.at[j, comp, pl.ds(w * size, size)],
                                sems.at[j, comp, w],
                            ).start()

    for j in range(count):
        pltpu.make_async_copy(
            tiles.at[j], tile_ref.at[:, pl.ds(j * rows, rows)], tile_sems.at[j]
        ).start()
    for j in range(count):
        edge = offs[j] == -2
        pltpu.make_async_copy(own.at[pl.ds(rows, PAD)], tails.at[j], tail_sems.at[j]).wait()
        tail = tails[j].astype(F32)
        low, high = tail[0:1, :size], tail[1:2, :size]
        seat = jnp.where(core == 0, high, 2.0 - high)
        pick = chosen(as_column(seat * size + low), 3 * size)
        for comp in range(3):

            @pl.when(jnp.logical_not(edge))
            def _(j=j, comp=comp):
                pltpu.make_async_copy(
                    own.at[pl.ds(0, size)], window.at[j, comp, pl.ds(0, size)], sems.at[j, comp, 0]
                ).wait()

            for w in range(1, 3):
                pltpu.make_async_copy(
                    own.at[pl.ds(0, size)], window.at[j, comp, pl.ds(w * size, size)], sems.at[j, comp, w]
                ).wait()
            at = j * rows + comp * size
            blocks[at : at + size] = dot(pick, window[j, comp]).astype(BF16)
    for j in range(count):
        pltpu.make_async_copy(
            tiles.at[j], tile_ref.at[:, pl.ds(j * rows, rows)], tile_sems.at[j]
        ).wait()
    outs = []
    for r in range(3):
        span = slice(r * size, (r + 1) * size)
        total_ref[span] = dot(tile_ref[span], blocks[...])
        here = pl.ds(r * size, size)
        outs.append(pltpu.make_async_copy(total_ref.at[here], total.at[here], out_sems.at[r]))
        outs[-1].start()
    for copy in outs:
        copy.wait()


def reduce_kernel(many_ref, sums, sums_ref, sem):
    total = many_ref[0]
    for i in range(1, many_ref.shape[0]):
        total += many_ref[i]
    for i in range(sums_ref.shape[0]):
        sums_ref[i] = total
    copy = pltpu.make_async_copy(sums_ref, sums, sem.at[0])
    copy.start()
    copy.wait()


def mix_kernel(
    clusters, planes, sc, near_col, near, sums, basis, mixed, tiles, thin, near_z, split,
    near_ref, sums_ref, basis_ref, mixed_ref, table_ref, stack_ref, coupled_ref, result,
    tile_ref, thin_ref, tail_ref, edge_ref, in_sems, sems, tile_sems, edge_sems,
):
    count, rows, _ = tiles.shape
    offs = offsets_of(clusters, sc, near_col, count)
    edges = [off == -2 for off in offs]
    some = functools.reduce(jnp.logical_or, edges)

    def edge_copies():
        return (
            pltpu.make_async_copy(thin, thin_ref, edge_sems.at[0]),
            pltpu.make_async_copy(near_z.at[pl.ds(rows, PAD)], tail_ref, edge_sems.at[1]),
        )

    def tile_copy(j):
        return pltpu.make_async_copy(tiles.at[j], tile_ref.at[j], tile_sems.at[j])

    pairs = ((sums, sums_ref), (basis, basis_ref), (near, near_ref), (mixed, mixed_ref))
    copies = [pltpu.make_async_copy(a, b, in_sems.at[i]) for i, (a, b) in enumerate(pairs)]
    for copy in copies:
        copy.start()

    @pl.when(some)
    def _():
        for copy in edge_copies():
            copy.start()

    for j in range(count):

        @pl.when(edges[j])
        def _(j=j):
            tile_copy(j).start()

    copies[0].wait()
    groups, rows, part = split.shape
    rank = sums_ref.shape[1]
    plane = sc[2]
    half = planes // 2
    other = jnp.where(plane < half, half, 0)
    for y in range(groups):
        lanes = slice(y * part, (y + 1) * part)
        base = y * 2 * planes
        coarse = sums_ref[base + 2 * other]
        for i in range(1, half):
            coarse += sums_ref[base + 2 * (other + i)]
        table_ref[:rank, lanes] = coarse
        for i in range(1, planes):
            at = lax.rem(plane + i, planes)
            table_ref[i * rank : (i + 1) * rank, lanes] = sums_ref[base + 2 * at + 1]
    table = table_ref[...]
    width = table.shape[0]
    high = table.astype(BF16)
    stack_ref[:width] = high
    stack_ref[width : 2 * width] = (table - high.astype(F32)).astype(BF16)
    stack_ref[2 * width :] = high
    copies[3].wait()
    step = mixed_ref.shape[0] // 2
    for i in range(2):
        span = slice(i * step, (i + 1) * step)
        coupled_ref[span] = dot(mixed_ref[span], stack_ref[...]).astype(BF16)
    copies[1].wait()
    copies[2].wait()
    size = rows // 3

    @pl.when(some)
    def _():
        for copy in edge_copies():
            copy.wait()
        tail = tail_ref[...].astype(F32)
        first = tail[1:2, :size] == jnp.where(sc[0] == 0, 0.0, 2.0)
        place = jnp.where(first, count_before(first.astype(F32)), -1.0)
        pick = chosen(as_column(place), size // 4)
        for comp in range(3):
            edge_ref[comp * size : (comp + 1) * size] = dot(pick, thin_ref[comp]).astype(BF16)

    for j in range(count):

        @pl.when(edges[j])
        def _(j=j):
            tile_copy(j).wait()
            for r in range(3):
                span = slice(r * size, (r + 1) * size)
                near_ref[span] += dot(tile_ref[j, span], edge_ref[...])

    outs = []
    for r in range(3):
        span = slice(r * size, (r + 1) * size)
        total = near_ref[span] + lax.dot_general(
            basis_ref[:, span], coupled_ref[...], (((0,), (0,)), ((), ())), preferred_element_type=F32
        )
        for i in range(groups):
            result[i, span] = total[:, i * part : (i + 1) * part].astype(BF16)
        here = pl.ds(r * size, size)
        outs.append(pltpu.make_async_copy(result.at[:, here], split.at[:, here], sems.at[r]))
        outs[-1].start()
    for copy in outs:
        copy.wait()


def last_kernel(arrived_ref, out_ref):
    total = arrived_ref[0].astype(F32)
    for i in range(1, arrived_ref.shape[0]):
        total += arrived_ref[i].astype(F32)
    out_ref[...] = total


def tie_kernel(*refs):
    del refs


def cost_of(flops):
    return pl.CostEstimate(flops=flops, bytes_accessed=10**6, transcendentals=0)


def tied(value, *after, flops=0):
    return pl.pallas_call(
        tie_kernel,
        out_shape=shape_of(value.shape, value.dtype),
        in_specs=[ANY] * (1 + len(after)),
        out_specs=ANY,
        input_output_aliases={0: 0},
        compiler_params=params(1),
        cost_estimate=cost_of(flops),
        name="tie",
    )(value, *after)


def in_hbm(*values):
    return [pltpu.with_memory_space_constraint(v, pltpu.MemorySpace.HBM) for v in values]


def shape_of(dims, dtype):
    return jax.ShapeDtypeStruct(dims, dtype)


def on_device(
    forces, order, bases, near_tiles, near_col, far_basis, far_coupling, far_scale, far_rank, far_target
):
    clusters = lax.axis_size(CLU)
    planes = lax.axis_size("clu_0")
    steps = lax.axis_size("clu_1")
    groups = lax.axis_size("grp")
    size = order.shape[0]
    comps, _, columns = forces.shape
    rows = comps * size
    part = columns // groups
    _, rank = bases.shape[:2]
    count = near_tiles.shape[1]
    far_count = far_target.shape[1]
    width = planes * rank
    sc = jnp.stack(
        [lax.axis_index("clu_2"), lax.axis_index("grp"), lax.axis_index("clu_0"), lax.axis_index(CLU)]
    ).astype(jnp.int32)

    def swapped(v):
        return lax.ppermute(v, "clu_2", [(0, 1), (1, 0)])

    def sent(v, by):
        pairs = [(i, (i + by if i % 2 else i - by) % clusters) for i in range(clusters)]
        return lax.ppermute(v, CLU, pairs)

    def exchanged(v, axis):
        return lax.all_to_all(v, axis, split_axis=0, concat_axis=0, tiled=True)

    chain = forces.reshape(rows, columns)
    halo, block = pl.pallas_call(
        functools.partial(dress_kernel, clusters),
        out_shape=(shape_of((rows + PAD, part), BF16), shape_of((rows + PAD, columns), BF16)),
        in_specs=[SMEM, HBM, HBM],
        out_specs=(VMEM, HBM),
        scratch_shapes=[
            pltpu.VMEM((1, size), jnp.int32),
            pltpu.VMEM((PAD, columns), BF16),
            pltpu.SemaphoreType.DMA((4,)),
        ],
        compiler_params=params(4),
        name="dress",
    )(sc, *in_hbm(order.reshape(1, size), chain))
    halo = sent(halo, 1)
    block = tied(block, flops=12 * 10**9)
    pair = swapped(block)
    near_z = sent(block, -2)
    far_z = sent(block, 2)

    keep, send = pl.pallas_call(
        pieces_kernel,
        out_shape=(shape_of((rank, part), F32),) * 2,
        in_specs=[SMEM, VMEM, VMEM, VMEM, VMEM],
        out_specs=(VMEM, VMEM),
        compiler_params=params(12),
        cost_estimate=cost_of(5 * 10**9),
        name="pieces",
    )(sc, halo, block, pair, bases.transpose(0, 2, 1, 3))
    level_sum = keep + swapped(send)
    many = exchanged(jnp.broadcast_to(level_sum, (steps, rank, part)), "clu_1")
    thin, mixed = pl.pallas_call(
        functools.partial(side_kernel, planes),
        out_shape=(
            shape_of((comps, size // 4, columns), BF16),
            shape_of((far_count * rank, 3 * width), BF16),
        ),
        in_specs=[SMEM, SMEM, SMEM, SMEM, HBM, HBM, VMEM, ANY],
        out_specs=(HBM, HBM),
        scratch_shapes=[
            pltpu.VMEM((far_count, rank, rank), BF16),
            pltpu.VMEM((rows, columns), BF16),
            pltpu.VMEM((far_count * rank, 3 * width), BF16),
            pltpu.VMEM((comps, size // 4, columns), BF16),
            pltpu.SemaphoreType.DMA((4,)),
        ],
        compiler_params=params(12),
        name="side",
    )(
        sc, *in_hbm(far_target[0], far_rank[0], far_scale[0], far_coupling[0], block), halo, level_sum,
    )
    many = tied(many, near_z, far_z, thin, mixed)
    thin = sent(thin, 3)
    pair_near = swapped(near_z)
    pair_far = swapped(far_z)
    fan = groups * 2 * planes
    sums = pl.pallas_call(
        reduce_kernel,
        out_shape=shape_of((fan, rank, part), F32),
        in_specs=[VMEM],
        out_specs=HBM,
        scratch_shapes=[pltpu.VMEM((fan, rank, part), F32), pltpu.SemaphoreType.DMA((1,))],
        compiler_params=params(4),
        name="reduce",
    )(many)
    sums = exchanged(sums, ("grp", "clu_0", "clu_2"))
    near = pl.pallas_call(
        functools.partial(near_kernel, clusters),
        out_shape=shape_of((rows, columns), F32),
        in_specs=[SMEM, SMEM, HBM] + [ANY] * 6,
        out_specs=HBM,
        scratch_shapes=[
            pltpu.VMEM((rows, count * rows), BF16),
            pltpu.VMEM((count, PAD, columns), BF16),
            pltpu.VMEM((count, comps, rows, columns), BF16),
            pltpu.VMEM((count * rows, columns), BF16),
            pltpu.VMEM((rows, columns), F32),
            pltpu.SemaphoreType.DMA((count, 3, 3)),
            pltpu.SemaphoreType.DMA((count,)),
            pltpu.SemaphoreType.DMA((count,)),
            pltpu.SemaphoreType.DMA((3,)),
        ],
        compiler_params=params(48),
        cost_estimate=cost_of(12 * 10**9),
        name="near",
    )(
        sc, *in_hbm(near_col[0], near_tiles[0]),
        *in_hbm(block, near_z), pair_far, *in_hbm(pair, far_z), pair_near,
    )
    split = pl.pallas_call(
        functools.partial(mix_kernel, clusters, planes),
        out_shape=shape_of((groups, rows, part), BF16),
        in_specs=[SMEM, SMEM, ANY, ANY, HBM, ANY, HBM, HBM, HBM],
        out_specs=HBM,
        scratch_shapes=[
            pltpu.VMEM((rows, columns), F32),
            pltpu.VMEM((fan, rank, part), F32),
            pltpu.VMEM((far_count * rank, rows), BF16),
            pltpu.VMEM((far_count * rank, 3 * width), BF16),
            pltpu.VMEM((width, columns), F32),
            pltpu.VMEM((3 * width, columns), BF16),
            pltpu.VMEM((far_count * rank, columns), BF16),
            pltpu.VMEM((groups, rows, part), BF16),
            pltpu.VMEM((count, rows, rows), BF16),
            pltpu.VMEM((comps, size // 4, columns), BF16),
            pltpu.VMEM((PAD, columns), BF16),
            pltpu.VMEM((rows, columns), BF16),
            pltpu.SemaphoreType.DMA((4,)),
            pltpu.SemaphoreType.DMA((3,)),
            pltpu.SemaphoreType.DMA((count,)),
            pltpu.SemaphoreType.DMA((2,)),
        ],
        compiler_params=params(24),
        name="mix",
    )(
        sc, *in_hbm(near_col[0]), near, sums, *in_hbm(far_basis.reshape(far_count * rank, rows)), mixed,
        *in_hbm(near_tiles[0], thin, near_z),
    )
    arrived = exchanged(split, "grp")
    velocity = pl.pallas_call(
        last_kernel,
        out_shape=shape_of((rows, part), F32),
        in_specs=[VMEM],
        out_specs=VMEM,
        compiler_params=params(4),
        name="last",
    )(arrived)
    return velocity.reshape(comps, size, part)


def solution(mesh):
    clusters = mesh.shape["clu"]
    torus = Mesh(
        mesh.devices.reshape(mesh.shape["grp"], 4, clusters // 8, 2),
        ("grp", "clu_0", "clu_1", "clu_2"),
    )
    in_specs = (
        P(None, CLU, None),
        P(CLU),
        P(None, None, None, CLU),
        P(CLU, "grp", None, None),
        P(CLU, "grp"),
        P(CLU, "grp", None, None),
        P(CLU, "grp", None, None),
        P(CLU, "grp"),
        P(CLU, "grp"),
        P(CLU, "grp"),
    )
    return jax.shard_map(
        on_device, mesh=torus, in_specs=in_specs, out_specs=P(None, CLU, "grp"), check_vma=False
    )
```

```python
import functools

import jax
import jax.numpy as jnp
from jax import lax
from jax.experimental import pallas as pl
from jax.experimental.pallas import tpu as pltpu
from jax.sharding import Mesh
from jax.sharding import PartitionSpec as P

CLU = ("clu_0", "clu_1", "clu_2")
PAD = 16
F32 = jnp.float32
BF16 = jnp.bfloat16
VMEM = pl.BlockSpec(memory_space=pltpu.VMEM)
SMEM = pl.BlockSpec(memory_space=pltpu.SMEM)
ANY = pl.BlockSpec(memory_space=pl.ANY)
HBM = pl.BlockSpec(memory_space=pltpu.MemorySpace.HBM)


def params(mib):
    return pltpu.CompilerParams(vmem_limit_bytes=mib * 2**20)


def iota(shape, dim):
    return lax.broadcasted_iota(jnp.int32, shape, dim)


def dot(a, b):
    return jnp.dot(a, b, preferred_element_type=F32)


def as_column(row):
    size = row.shape[1]
    square = (size, size)
    spread = jnp.where(iota(square, 0) == iota(square, 1), jnp.broadcast_to(row, square), 0.0)
    return jnp.sum(spread, axis=1, keepdims=True)


def count_before(mask):
    size = mask.shape[1]
    square = (size, size)
    upto = (iota(square, 0) <= iota(square, 1)).astype(F32).astype(BF16)
    rows = jnp.broadcast_to(mask, (16, size)).astype(BF16)
    return dot(rows, upto)[:1] - 1.0


def chosen(column, width):
    shape = (column.shape[0], width)
    return (jnp.broadcast_to(column, shape) == iota(shape, 1).astype(F32)).astype(F32).astype(BF16)


def rows_of(v, width):
    return [v[:, i : i + width] for i in range(0, v.shape[1], width)]


def stacked(lines, width):
    at = iota((PAD, width), 0)
    out = jnp.zeros((PAD, width), F32)
    for i, v in enumerate(lines):
        if v.shape[1] < width:
            v = jnp.concatenate([v, jnp.zeros((1, width - v.shape[1]), F32)], axis=1)
        out = jnp.where(at == i, v, out)
    return out.astype(BF16)


def dress_kernel(clusters, sc, order, forces, halo_ref, block, order_ref, lines_ref, sems):
    rows, columns = forces.shape
    size = order.shape[1]
    part = halo_ref.shape[1]
    start = pl.multiple_of(sc[1] * part, part)
    copies = [
        pltpu.make_async_copy(order, order_ref, sems.at[0]),
        pltpu.make_async_copy(forces.at[:, pl.ds(start, part)], halo_ref.at[pl.ds(0, rows)], sems.at[1]),
        pltpu.make_async_copy(forces, block.at[pl.ds(0, rows)], sems.at[2]),
    ]
    for copy in copies:
        copy.start()
    copies[0].wait()
    rel = order_ref[...] - (sc[3] - 1) * size
    rel = jnp.where(rel < 0, rel + clusters * size, rel)
    rel = jnp.where(rel >= clusters * size, rel - clusters * size, rel)
    high = (rel >= size).astype(jnp.int32) + (rel >= 2 * size).astype(jnp.int32)
    low = (rel - high * size).astype(F32)
    high = high.astype(F32)
    lines_ref[...] = stacked([low, high], columns)
    copy = pltpu.make_async_copy(lines_ref, block.at[pl.ds(rows, PAD)], sems.at[3])
    copy.start()
    halo_ref[rows:] = stacked(rows_of(low, part) + rows_of(high, part), part)
    copy.wait()
    copies[1].wait()
    copies[2].wait()


def pieces_kernel(sc, halo_ref, own_ref, pair_ref, bases_ref, keep_ref, send_ref):
    levels, comps, rank, size = bases_ref.shape
    rows = comps * size
    part = halo_ref.shape[1]
    core = sc[0]
    start = pl.multiple_of(sc[1] * part, part)
    tail = own_ref[rows:].astype(F32)
    low, high = tail[0:1, :size], tail[1:2, :size]
    seat = jnp.where(core == 0, high, 2.0 - high)
    pick = chosen(as_column(seat * size + low), 3 * size)
    sums = [jnp.zeros((rank, part), F32) for _ in range(levels)]
    for comp in range(comps):
        span = slice(comp * size, (comp + 1) * size)
        got = dot(pick[:, :size], halo_ref[span])
        got += dot(pick[:, size : 2 * size], own_ref[span, pl.ds(start, part)])
        got += dot(pick[:, 2 * size :], pair_ref[span, pl.ds(start, part)])
        got = got.astype(BF16)
        for level in range(levels):
            sums[level] += dot(bases_ref[level, comp], got)
    keep_ref[...] = jnp.where(core == 0, sums[0], sums[1])
    send_ref[...] = jnp.where(core == 0, sums[1], sums[0])


def side_kernel(
    planes, sc, target, keeps, scale, coupling, own, halo_ref, after, thin, mixed,
    coupling_ref, own_ref, mixed_ref, thin_ref, sems,
):
    del after
    copy = pltpu.make_async_copy(coupling, coupling_ref, sems.at[0])
    copy.start()
    own_copy = pltpu.make_async_copy(own.at[pl.ds(0, own_ref.shape[0])], own_ref, sems.at[3])
    own_copy.start()
    comps, quarter, _ = thin.shape
    size = 4 * quarter
    rows = comps * size
    part = halo_ref.shape[1]
    core = sc[0]
    tail = halo_ref[rows:].astype(F32)
    per = size // part
    low = jnp.concatenate([tail[i : i + 1] for i in range(per)], axis=1)
    high = jnp.concatenate([tail[per + i : per + i + 1] for i in range(per)], axis=1)
    mine = high == jnp.where(core == 0, 2.0, 0.0)
    place = count_before(mine.astype(F32))
    shape = (quarter, size)
    seats = jnp.broadcast_to(jnp.where(mine, place, -1.0), shape)
    into = (seats == iota(shape, 0).astype(F32)).astype(F32).astype(BF16)
    pack = dot(into, chosen(as_column(low), size)).astype(BF16)
    own_copy.wait()
    for comp in range(comps):
        thin_ref[comp] = dot(pack, own_ref[comp * size : (comp + 1) * size]).astype(BF16)
    thin_copy = pltpu.make_async_copy(thin_ref, thin, sems.at[1])
    thin_copy.start()
    copy.wait()
    blocks, rank, _ = coupling_ref.shape
    width = mixed_ref.shape[1] // 3
    lane = iota((rank, width), 1)
    for b in range(blocks):
        goal = target[b]
        first = jnp.where(goal < 2, 0, lax.rem(goal - 2 - sc[2] + planes, planes)) * rank
        tile = coupling_ref[b].astype(F32) * scale[b]
        tile = jnp.concatenate([tile] * (width // rank), axis=1)
        tile = jnp.where((lane >= first) & (lane < first + keeps[b]), tile, 0.0)
        high = tile.astype(BF16)
        at = slice(b * rank, (b + 1) * rank)
        mixed_ref[at, :width] = high
        mixed_ref[at, width : 2 * width] = high
        mixed_ref[at, 2 * width :] = (tile - high.astype(F32)).astype(BF16)
    copy = pltpu.make_async_copy(mixed_ref, mixed, sems.at[2])
    copy.start()
    copy.wait()
    thin_copy.wait()


def offsets_of(clusters, sc, near_col, count):
    offs = []
    for j in range(count):
        off = near_col[j] - sc[3] + 2
        off = jnp.where(off < 0, off + clusters, off)
        off = jnp.where(off >= clusters, off - clusters, off) - 2
        offs.append(jnp.where(sc[0] == 0, off, -off))
    return offs


def near_kernel(
    clusters, sc, near_col, tiles, own, near_z, pair_far, pair, far_z, pair_near,
    total, tile_ref, tails, window, blocks, total_ref, sems, tail_sems, tile_sems, out_sems,
):
    count, rows, _ = tiles.shape
    columns = own.shape[1]
    size = rows // 3
    core = sc[0]
    seats = (None, near_z, pair_far, own, pair, far_z, pair_near)
    offs = offsets_of(clusters, sc, near_col, count)
    for j in range(count):
        for o in range(-2, 3):

            @pl.when(offs[j] == o)
            def _(j=j, o=o):
                pltpu.make_async_copy(seats[o + 3].at[pl.ds(rows, PAD)], tails.at[j], tail_sems.at[j]).start()
                for comp in range(3):
                    for w in range(3):
                        source = seats[o + 2 + w]
                        if source is None:
                            window[j, comp, :size] = jnp.zeros((size, columns), BF16)
                        else:
                            pltpu.make_async_copy(
                                source.at[pl.ds(comp * size, size)],
                                window.at[j, comp, pl.ds(w * size, size)],
                                sems.at[j, comp, w],
                            ).start()

    for j in range(count):
        pltpu.make_async_copy(
            tiles.at[j], tile_ref.at[:, pl.ds(j * rows, rows)], tile_sems.at[j]
        ).start()
    for j in range(count):
        edge = offs[j] == -2
        pltpu.make_async_copy(own.at[pl.ds(rows, PAD)], tails.at[j], tail_sems.at[j]).wait()
        tail = tails[j].astype(F32)
        low, high = tail[0:1, :size], tail[1:2, :size]
        seat = jnp.where(core == 0, high, 2.0 - high)
        pick = chosen(as_column(seat * size + low), 3 * size)
        for comp in range(3):

            @pl.when(jnp.logical_not(edge))
            def _(j=j, comp=comp):
                pltpu.make_async_copy(
                    own.at[pl.ds(0, size)], window.at[j, comp, pl.ds(0, size)], sems.at[j, comp, 0]
                ).wait()

            for w in range(1, 3):
                pltpu.make_async_copy(
                    own.at[pl.ds(0, size)], window.at[j, comp, pl.ds(w * size, size)], sems.at[j, comp, w]
                ).wait()
            at = j * rows + comp * size
            blocks[at : at + size] = dot(pick, window[j, comp]).astype(BF16)
    for j in range(count):
        pltpu.make_async_copy(
            tiles.at[j], tile_ref.at[:, pl.ds(j * rows, rows)], tile_sems.at[j]
        ).wait()
    outs = []
    for r in range(3):
        span = slice(r * size, (r + 1) * size)
        total_ref[span] = dot(tile_ref[span], blocks[...])
        here = pl.ds(r * size, size)
        outs.append(pltpu.make_async_copy(total_ref.at[here], total.at[here], out_sems.at[r]))
        outs[-1].start()
    for copy in outs:
        copy.wait()


def reduce_kernel(many_ref, sums, sums_ref, sem):
    total = many_ref[0]
    for i in range(1, many_ref.shape[0]):
        total += many_ref[i]
    for i in range(sums_ref.shape[0]):
        sums_ref[i] = total
    copy = pltpu.make_async_copy(sums_ref, sums, sem.at[0])
    copy.start()
    copy.wait()


def mix_kernel(
    clusters, planes, sc, near_col, near, sums, basis, mixed, tiles, thin, near_z, split,
    near_ref, sums_ref, basis_ref, mixed_ref, table_ref, stack_ref, coupled_ref, result,
    tile_ref, thin_ref, tail_ref, edge_ref, in_sems, sems, tile_sems, edge_sems,
):
    count, rows, _ = tiles.shape
    offs = offsets_of(clusters, sc, near_col, count)
    edges = [off == -2 for off in offs]
    some = functools.reduce(jnp.logical_or, edges)

    def edge_copies():
        return (
            pltpu.make_async_copy(thin, thin_ref, edge_sems.at[0]),
            pltpu.make_async_copy(near_z.at[pl.ds(rows, PAD)], tail_ref, edge_sems.at[1]),
        )

    def tile_copy(j):
        return pltpu.make_async_copy(tiles.at[j], tile_ref.at[j], tile_sems.at[j])

    pairs = ((sums, sums_ref), (basis, basis_ref), (near, near_ref), (mixed, mixed_ref))
    copies = [pltpu.make_async_copy(a, b, in_sems.at[i]) for i, (a, b) in enumerate(pairs)]
    for copy in copies:
        copy.start()

    @pl.when(some)
    def _():
        for copy in edge_copies():
            copy.start()

    for j in range(count):

        @pl.when(edges[j])
        def _(j=j):
            tile_copy(j).start()

    copies[0].wait()
    groups, rows, part = split.shape
    rank = sums_ref.shape[1]
    plane = sc[2]
    half = planes // 2
    other = jnp.where(plane < half, half, 0)
    for y in range(groups):
        lanes = slice(y * part, (y + 1) * part)
        base = y * 2 * planes
        coarse = sums_ref[base + 2 * other]
        for i in range(1, half):
            coarse += sums_ref[base + 2 * (other + i)]
        table_ref[:rank, lanes] = coarse
        for i in range(1, planes):
            at = lax.rem(plane + i, planes)
            table_ref[i * rank : (i + 1) * rank, lanes] = sums_ref[base + 2 * at + 1]
    table = table_ref[...]
    width = table.shape[0]
    high = table.astype(BF16)
    stack_ref[:width] = high
    stack_ref[width : 2 * width] = (table - high.astype(F32)).astype(BF16)
    stack_ref[2 * width :] = high
    copies[3].wait()
    step = mixed_ref.shape[0] // 2
    for i in range(2):
        span = slice(i * step, (i + 1) * step)
        coupled_ref[span] = dot(mixed_ref[span], stack_ref[...]).astype(BF16)
    copies[1].wait()
    copies[2].wait()
    size = rows // 3

    @pl.when(some)
    def _():
        for copy in edge_copies():
            copy.wait()
        tail = tail_ref[...].astype(F32)
        first = tail[1:2, :size] == jnp.where(sc[0] == 0, 0.0, 2.0)
        place = jnp.where(first, count_before(first.astype(F32)), -1.0)
        pick = chosen(as_column(place), size // 4)
        for comp in range(3):
            edge_ref[comp * size : (comp + 1) * size] = dot(pick, thin_ref[comp]).astype(BF16)

    for j in range(count):

        @pl.when(edges[j])
        def _(j=j):
            tile_copy(j).wait()
            for r in range(3):
                span = slice(r * size, (r + 1) * size)
                near_ref[span] += dot(tile_ref[j, span], edge_ref[...])

    outs = []
    for r in range(3):
        span = slice(r * size, (r + 1) * size)
        total = near_ref[span] + lax.dot_general(
            basis_ref[:, span], coupled_ref[...], (((0,), (0,)), ((), ())), preferred_element_type=F32
        )
        for i in range(groups):
            result[i, span] = total[:, i * part : (i + 1) * part].astype(BF16)
        here = pl.ds(r * size, size)
        outs.append(pltpu.make_async_copy(result.at[:, here], split.at[:, here], sems.at[r]))
        outs[-1].start()
    for copy in outs:
        copy.wait()


def last_kernel(arrived_ref, out_ref):
    total = arrived_ref[0].astype(F32)
    for i in range(1, arrived_ref.shape[0]):
        total += arrived_ref[i].astype(F32)
    out_ref[...] = total


def tie_kernel(*refs):
    del refs


def cost_of(flops):
    return pl.CostEstimate(flops=flops, bytes_accessed=10**6, transcendentals=0)


def tied(value, *after, flops=0):
    return pl.pallas_call(
        tie_kernel,
        out_shape=shape_of(value.shape, value.dtype),
        in_specs=[ANY] * (1 + len(after)),
        out_specs=ANY,
        input_output_aliases={0: 0},
        compiler_params=params(1),
        cost_estimate=cost_of(flops),
        name="tie",
    )(value, *after)


def in_hbm(*values):
    return [pltpu.with_memory_space_constraint(v, pltpu.MemorySpace.HBM) for v in values]


def shape_of(dims, dtype):
    return jax.ShapeDtypeStruct(dims, dtype)


def on_device(
    forces, order, bases, near_tiles, near_col, far_basis, far_coupling, far_scale, far_rank, far_target
):
    clusters = lax.axis_size(CLU)
    planes = lax.axis_size("clu_0")
    steps = lax.axis_size("clu_1")
    groups = lax.axis_size("grp")
    size = order.shape[0]
    comps, _, columns = forces.shape
    rows = comps * size
    part = columns // groups
    _, rank = bases.shape[:2]
    count = near_tiles.shape[1]
    far_count = far_target.shape[1]
    width = planes * rank
    sc = jnp.stack(
        [lax.axis_index("clu_2"), lax.axis_index("grp"), lax.axis_index("clu_0"), lax.axis_index(CLU)]
    ).astype(jnp.int32)

    def swapped(v):
        return lax.ppermute(v, "clu_2", [(0, 1), (1, 0)])

    def sent(v, by):
        pairs = [(i, (i + by if i % 2 else i - by) % clusters) for i in range(clusters)]
        return lax.ppermute(v, CLU, pairs)

    def exchanged(v, axis):
        return lax.all_to_all(v, axis, split_axis=0, concat_axis=0, tiled=True)

    chain = forces.reshape(rows, columns)
    halo, block = pl.pallas_call(
        functools.partial(dress_kernel, clusters),
        out_shape=(shape_of((rows + PAD, part), BF16), shape_of((rows + PAD, columns), BF16)),
        in_specs=[SMEM, HBM, HBM],
        out_specs=(VMEM, HBM),
        scratch_shapes=[
            pltpu.VMEM((1, size), jnp.int32),
            pltpu.VMEM((PAD, columns), BF16),
            pltpu.SemaphoreType.DMA((4,)),
        ],
        compiler_params=params(4),
        name="dress",
    )(sc, *in_hbm(order.reshape(1, size), chain))
    halo = sent(halo, 1)
    block = tied(block, flops=12 * 10**9)
    pair = swapped(block)
    near_z = sent(block, -2)
    far_z = sent(block, 2)

    keep, send = pl.pallas_call(
        pieces_kernel,
        out_shape=(shape_of((rank, part), F32),) * 2,
        in_specs=[SMEM, VMEM, VMEM, VMEM, VMEM],
        out_specs=(VMEM, VMEM),
        compiler_params=params(12),
        cost_estimate=cost_of(5 * 10**9),
        name="pieces",
    )(sc, halo, block, pair, bases.transpose(0, 2, 1, 3))
    level_sum = keep + swapped(send)
    many = exchanged(jnp.broadcast_to(level_sum, (steps, rank, part)), "clu_1")
    thin, mixed = pl.pallas_call(
        functools.partial(side_kernel, planes),
        out_shape=(
            shape_of((comps, size // 4, columns), BF16),
            shape_of((far_count * rank, 3 * width), BF16),
        ),
        in_specs=[SMEM, SMEM, SMEM, SMEM, HBM, HBM, VMEM, ANY],
        out_specs=(HBM, HBM),
        scratch_shapes=[
            pltpu.VMEM((far_count, rank, rank), BF16),
            pltpu.VMEM((rows, columns), BF16),
            pltpu.VMEM((far_count * rank, 3 * width), BF16),
            pltpu.VMEM((comps, size // 4, columns), BF16),
            pltpu.SemaphoreType.DMA((4,)),
        ],
        compiler_params=params(12),
        name="side",
    )(
        sc, *in_hbm(far_target[0], far_rank[0], far_scale[0], far_coupling[0], block), halo, level_sum,
    )
    near_z = tied(near_z, thin, mixed)
    far_z = tied(far_z, thin, mixed)
    many = tied(many, near_z, far_z)
    thin = sent(thin, 3)
    pair_near = swapped(near_z)
    pair_far = swapped(far_z)
    fan = groups * 2 * planes
    sums = pl.pallas_call(
        reduce_kernel,
        out_shape=shape_of((fan, rank, part), F32),
        in_specs=[VMEM],
        out_specs=HBM,
        scratch_shapes=[pltpu.VMEM((fan, rank, part), F32), pltpu.SemaphoreType.DMA((1,))],
        compiler_params=params(4),
        name="reduce",
    )(many)
    sums = exchanged(sums, ("grp", "clu_0", "clu_2"))
    near = pl.pallas_call(
        functools.partial(near_kernel, clusters),
        out_shape=shape_of((rows, columns), F32),
        in_specs=[SMEM, SMEM, HBM] + [ANY] * 6,
        out_specs=HBM,
        scratch_shapes=[
            pltpu.VMEM((rows, count * rows), BF16),
            pltpu.VMEM((count, PAD, columns), BF16),
            pltpu.VMEM((count, comps, rows, columns), BF16),
            pltpu.VMEM((count * rows, columns), BF16),
            pltpu.VMEM((rows, columns), F32),
            pltpu.SemaphoreType.DMA((count, 3, 3)),
            pltpu.SemaphoreType.DMA((count,)),
            pltpu.SemaphoreType.DMA((count,)),
            pltpu.SemaphoreType.DMA((3,)),
        ],
        compiler_params=params(48),
        cost_estimate=cost_of(4 * 10**9),
        name="near",
    )(
        sc, *in_hbm(near_col[0], near_tiles[0]),
        *in_hbm(block, near_z), pair_far, *in_hbm(pair, far_z), pair_near,
    )
    split = pl.pallas_call(
        functools.partial(mix_kernel, clusters, planes),
        out_shape=shape_of((groups, rows, part), BF16),
        in_specs=[SMEM, SMEM, HBM, ANY, HBM, ANY, HBM, HBM, HBM],
        out_specs=HBM,
        scratch_shapes=[
            pltpu.VMEM((rows, columns), F32),
            pltpu.VMEM((fan, rank, part), F32),
            pltpu.VMEM((far_count * rank, rows), BF16),
            pltpu.VMEM((far_count * rank, 3 * width), BF16),
            pltpu.VMEM((width, columns), F32),
            pltpu.VMEM((3 * width, columns), BF16),
            pltpu.VMEM((far_count * rank, columns), BF16),
            pltpu.VMEM((groups, rows, part), BF16),
            pltpu.VMEM((count, rows, rows), BF16),
            pltpu.VMEM((comps, size // 4, columns), BF16),
            pltpu.VMEM((PAD, columns), BF16),
            pltpu.VMEM((rows, columns), BF16),
            pltpu.SemaphoreType.DMA((4,)),
            pltpu.SemaphoreType.DMA((3,)),
            pltpu.SemaphoreType.DMA((count,)),
            pltpu.SemaphoreType.DMA((2,)),
        ],
        compiler_params=params(24),
        name="mix",
    )(
        sc, *in_hbm(near_col[0], near), sums, *in_hbm(far_basis.reshape(far_count * rank, rows)), mixed,
        *in_hbm(near_tiles[0], thin, near_z),
    )
    arrived = exchanged(split, "grp")
    velocity = pl.pallas_call(
        last_kernel,
        out_shape=shape_of((rows, part), F32),
        in_specs=[VMEM],
        out_specs=VMEM,
        compiler_params=params(4),
        name="last",
    )(arrived)
    return velocity.reshape(comps, size, part)


def solution(mesh):
    clusters = mesh.shape["clu"]
    torus = Mesh(
        mesh.devices.reshape(mesh.shape["grp"], 4, clusters // 8, 2),
        ("grp", "clu_0", "clu_1", "clu_2"),
    )
    in_specs = (
        P(None, CLU, None),
        P(CLU),
        P(None, None, None, CLU),
        P(CLU, "grp", None, None),
        P(CLU, "grp"),
        P(CLU, "grp", None, None),
        P(CLU, "grp", None, None),
        P(CLU, "grp"),
        P(CLU, "grp"),
        P(CLU, "grp"),
    )
    return jax.shard_map(
        on_device, mesh=torus, in_specs=in_specs, out_specs=P(None, CLU, "grp"), check_vma=False
    )
```
